32 devices in a mesh: shot: 2 (over x), strip: 16 (over z, y, core).
Axes of the slice: x: 2, y: 2, z: 4, core: 2. Of those that a mesh axis runs over, the one named last changes fastest.
Arguments:
- waves: float32 [2, 2, 8, 512, 512], P(None, None, 'shot', 'strip'), parts along dimension 2, may hold values from -6 to 6
- levels: int32 [512, 512], P('strip'), may hold values from 0 to 4
- coeffs: float32 [2, 4, 5, 17], replicated, may hold values from -0.7 to 0.7
- angles: float32 [4, 5], replicated, may hold values from -3.140625 to 3.140625
- order: int32 [8], P('shot'), parts along dimension 0, may hold values from 0 to 3, each once
Outputs:
- waves_out: float32 [2, 2, 8, 512, 512], P(None, None, 'shot', 'strip'), parts along dimension 2
- image: float32 [4, 512, 512], P('shot', 'strip'), parts along dimension 0
The draws below stay inside these ranges and needn't reach their ends.
There are 2 independent parts, one for each index of `shot`. The reference program is written for one: setup_inputs(seed, part) draws one part's arguments, and reference() takes and returns one part's arrays. A program takes and returns all parts, laid end to end along the dimension named above; an argument that names none is the same for every part. Nothing has to cross between parts.
Inputs may be any that keep to these rules, and one draw needn't show every extreme that they name: order names every table row once.
All inputs are finite; a program needn't handle non-finite values.
Results may differ from the reference program's by a relative error of at most 0.00013.
Values sent between devices are 32-bit elements; how exact they have to be, the bound alone decides.
No kernel may reach another device: no remote copies, remote signals or barrier semaphores. Data moves between devices by JAX's collectives and lax.ppermute only.
A program may use at most 64 MiB of HBM per device.

```python
import jax
import jax.numpy as jnp
from jax import lax

INLINE = 512
FREQ = 4
LEVELS = 5
TAPS = 17
STEPS = 2
CROSS = 512


def set_ends(array, key, least, top_value):
    longest = array.shape.index(max(array.shape))
    spots = []
    for shift in (0, 1):
        where = [jax.random.randint(jax.random.fold_in(key, axis), (), 0, length) for axis, length in enumerate(array.shape)]
        where[longest] = (where[longest] + shift) % array.shape[longest]
        spots.append(tuple(where))
    return array.at[spots[0]].set(least).at[spots[1]].set(top_value)


def steps_of(rng, dims, split, smallest, high):
    factor_of = 1.0
    for position, shards_of in split:
        heights = jax.random.uniform(jax.random.fold_in(jax.random.fold_in(rng, 6), position), (shards_of,), jnp.float32, smallest / len(split), high / len(split))
        factor_of = factor_of * jnp.repeat(jnp.exp(heights), dims[position] // shards_of).reshape((-1,) + (1,) * (len(dims) - 1 - position))
    return factor_of


def gaussian(rng, shape, scale, most, split=(), kind=jnp.bfloat16):
    entries = scale * jax.random.normal(rng, shape, jnp.float32)
    if split:
        entries = entries * steps_of(rng, shape, split, -0.22, 0.18)
    return jnp.clip(entries, -most, most).astype(kind)


def setup_inputs(seed: int = 0, part: int = 0) -> dict:
    key_of = jax.random.split(jax.random.key(seed), 6)
    part_keys = jax.random.split(jax.random.fold_in(key_of[5], part), 6)
    waves = gaussian(part_keys[0], (2, 2, FREQ, CROSS, INLINE), 1.0, 6.0, ((3, 16),), jnp.float32)
    levels = set_ends(jax.random.randint(key_of[1], (CROSS, INLINE), 0, LEVELS), jax.random.fold_in(key_of[1], 1), 0, LEVELS - 1).astype(jnp.int32)
    coeffs = gaussian(key_of[2], (2, FREQ, LEVELS, TAPS), 0.17, 0.7, (), jnp.float32)
    angles = jnp.clip(jax.random.uniform(key_of[3], (FREQ, LEVELS), jnp.float32, -3.140625, 3.140625), -3.140625, 3.140625)
    order = jax.random.permutation(part_keys[4], FREQ).astype(jnp.int32)
    return {"waves": waves, "levels": levels, "coeffs": coeffs, "angles": angles, "order": order}


def one_pass(field_real, field_imag, coef_table, levels, along_axis, conj_sign, half_taps):
    widths = [(0, 0), (0, 0), (0, 0)]
    widths[along_axis] = (half_taps, half_taps)
    pad_real = jnp.pad(field_real, widths)
    pad_imag = jnp.pad(field_imag, widths)
    out_length = field_real.shape[along_axis]
    acc_real = jnp.zeros(field_real.shape, jnp.float32)
    acc_imag = jnp.zeros(field_real.shape, jnp.float32)
    for tap_index in range(2 * half_taps + 1):
        shift_real = lax.slice_in_dim(pad_real, tap_index, tap_index + out_length, axis=along_axis)
        shift_imag = lax.slice_in_dim(pad_imag, tap_index, tap_index + out_length, axis=along_axis)
        coef_real = coef_table[0][:, levels, tap_index]
        coef_imag = coef_table[1][:, levels, tap_index] * conj_sign
        acc_real = acc_real + (coef_real * shift_real - coef_imag * shift_imag)
        acc_imag = acc_imag + (coef_real * shift_imag + coef_imag * shift_real)
    return acc_real, acc_imag


def reference(waves, levels, coeffs, angles, order):
    coef_table = coeffs[:, order]
    turn_table = angles[order]
    phase_angle = turn_table[:, levels]
    cosine = jnp.cos(phase_angle)
    sine_part = jnp.sin(phase_angle)
    half_taps = (coeffs.shape[3] - 1) // 2
    source_real, source_imag = waves[0, 0], waves[0, 1]
    receiver_real, receiver_imag = waves[1, 0], waves[1, 1]
    slabs = []
    for depth_step in range(STEPS):
        source_real, source_imag = (source_real * cosine - source_imag * sine_part,
                                    source_real * sine_part + source_imag * cosine)
        receiver_real, receiver_imag = (receiver_real * cosine + receiver_imag * sine_part,
                                        -receiver_real * sine_part + receiver_imag * cosine)
        for along_axis in (2, 1):
            source_real, source_imag = one_pass(source_real, source_imag, coef_table, levels, along_axis, 1.0, half_taps)
            receiver_real, receiver_imag = one_pass(receiver_real, receiver_imag, coef_table, levels, along_axis, -1.0, half_taps)
        slabs.append(jnp.sum(source_real * receiver_real + source_imag * receiver_imag, axis=0))
    waves_out = jnp.stack([jnp.stack([source_real, source_imag]), jnp.stack([receiver_real, receiver_imag])])
    return waves_out, jnp.stack(slabs)
```

```python
import functools

import jax
import jax.numpy as jnp
from jax import lax
from jax.experimental import pallas as pl
from jax.experimental.pallas import tpu as pltpu
from jax.sharding import PartitionSpec as P

STEPS = 2
LANES = 128
F32 = jnp.float32
BF16 = jnp.bfloat16


def pick(values, masks):
    out = values[0]
    for value, mask in zip(values[1:], masks):
        out = jnp.where(mask, value, out)
    return out


def level_masks(level, count):
    return [level == float(l) for l in range(1, count)]


def split(cells):
    high = cells.astype(BF16)
    return high, (cells - high.astype(F32)).astype(BF16)


def build_filters(coef_ref, order_ref, pad_ref, lhs_ref, block):
    freqs, rows, _ = lhs_ref.shape
    levels, taps = coef_ref.shape[2:]
    pad_ref[...] = jnp.zeros_like(pad_ref)
    pad_ref[:, :, :levels, :taps] = coef_ref[...]
    wide = 2 * block

    def body(f, carry):
        row = order_ref[f]
        real, imag = pad_ref[0, row], pad_ref[1, row]
        tables = (real - pltpu.roll(imag, wide, 1), imag + pltpu.roll(real, wide, 1))
        for level in range(levels):
            for part in range(2):
                line = jnp.broadcast_to(tables[part][level : level + 1], (block, LANES))
                band = pltpu.roll(line, 0, 1, stride=1, stride_axis=0)
                high, low = split(band)
                high = high.astype(F32)
                at = (level * 2 + part) * block
                lhs_ref[f, at : at + block, :LANES] = (high + pltpu.roll(high, 2 * wide, 1)).astype(BF16)
                lhs_ref[f, at : at + block, LANES:] = low
        return carry

    lax.fori_loop(0, freqs, body, 0)


def apply_band(lhs, reals, imags, masks, block):
    rhs = jnp.concatenate([reals[0], imags[0], reals[1], imags[1], reals[0], imags[0]], axis=0)
    found = jnp.dot(lhs[:, : rhs.shape[0]], rhs, preferred_element_type=F32)
    count = found.shape[0] // (2 * block)
    return [
        pick([found[(l * 2 + part) * block : (l * 2 + part + 1) * block] for l in range(count)], masks)
        for part in range(2)
    ]


def turn_tables(cs_ref, row, masks):
    count = len(masks) + 1
    return [
        pick([jnp.full(masks[0].shape, cs_ref[part, row, l], F32) for l in range(count)], masks)
        for part in range(2)
    ]


def rotate(cells, cosine, sine):
    real, imag = cells
    return real * cosine - imag * sine, real * sine + imag * cosine


def to_columns(fields, block):
    chunks = fields[0].shape[1] // LANES
    return jnp.concatenate(
        [field[:, c * LANES : (c + 1) * LANES] for c in range(chunks) for field in fields], axis=0
    ).T


def inline(lhs, fields, masks_t, block):
    half = block // 2
    count = len(fields)
    chunks = fields[0][0].shape[1] // LANES
    step = count * block
    lane = lax.broadcasted_iota(jnp.int32, (half, LANES), 1)
    parts = []
    for part in range(2):
        cols = to_columns([field[part] for field in fields], block)
        before = jnp.where(lane < step, 0.0, pltpu.roll(cols[LANES - half :], step, 1))
        after = jnp.where(lane >= LANES - step, 0.0, pltpu.roll(cols[:half], LANES - step, 1))
        parts.append(split(jnp.concatenate([before, cols, after], axis=0)))
    mid = LANES // 2
    halves = [[[], []], [[], []]]
    for at in range(0, mid, block):
        windows = [
            [
                jnp.concatenate([x[at : at + 2 * block], x[mid + at : mid + at + 2 * block]], axis=1)
                for x in parts[part]
            ]
            for part in range(2)
        ]
        masks = [jnp.concatenate([m[at : at + block], m[mid + at : mid + at + block]], axis=1) for m in masks_t]
        got = apply_band(lhs, windows[0], windows[1], masks, block)
        for part in range(2):
            halves[part][0].append(got[part][:, :LANES])
            halves[part][1].append(got[part][:, LANES:])
    back = [jnp.concatenate(halves[part][0] + halves[part][1], axis=0).T for part in range(2)]
    return [
        [
            jnp.concatenate(
                [back[part][(c * count + i) * block : (c * count + i + 1) * block] for c in range(chunks)], axis=1
            )
            for part in range(2)
        ]
        for i in range(count)
    ]


def store_split(ref, lead, fields):
    for i, field in enumerate(fields):
        for part in range(2):
            high, low = split(field[part])
            ref[lead + (i, 0, part)] = high
            ref[lead + (i, 1, part)] = low


def crossline(lhs, win_ref, first, second, f, masks, block):
    wide = 2 * LANES
    width = win_ref.shape[-1]
    fields = []
    for i in range(2):
        pieces = [[], []]
        for at in range(0, width, wide):
            windows = [
                [
                    jnp.concatenate(
                        [win_ref[slot, f, i, kind, part, :, at : at + wide] for slot in (first, second)], axis=0
                    )
                    for kind in range(2)
                ]
                for part in range(2)
            ]
            got = apply_band(lhs, windows[0], windows[1], [m[:, at : at + wide] for m in masks], block)
            for part in range(2):
                pieces[part].append(got[part])
        fields.append([jnp.concatenate(p, axis=1) for p in pieces])
    return fields


def image_of(fields):
    (sr, si), (qr, qi) = fields
    return sr * qr - si * qi


def first_kernel(
    half_ref, order_ref, cs_ref, coef_ref, waves_ref, lev_ref, fast_ref,
    out_ref, img_ref, edge_ref, mid_ref, lhs_ref,
    pad_ref, win_ref, next_ref, levw_ref, levt_ref, done_ref, acc_ref, sem,
):
    freqs = lhs_ref.shape[0]
    levels, taps = coef_ref.shape[2:]
    block = taps - 1
    half = block // 2
    rows = lev_ref.shape[0]
    c = half_ref[0]
    build_filters(coef_ref, order_ref, pad_ref, lhs_ref, block)
    own = lev_ref[...].astype(F32)
    fast_plane = fast_ref.shape[0] - 1
    levw_ref[pl.ds(pl.multiple_of(block * c, block), block)] = jnp.where(c == 0, own[block:], own[:block])
    levw_ref[pl.ds(pl.multiple_of(block * (1 - c), block), block)] = fast_ref[fast_plane]
    img_ref[...] = jnp.zeros_like(img_ref)
    acc_ref[...] = jnp.zeros_like(acc_ref)

    def column_levels(lev):
        levt_ref[...] = to_columns([lev, lev], block)

    for slot in range(3):
        if slot < 2:
            lev = own[slot * block : (slot + 1) * block]
        else:
            lev = fast_ref[fast_plane]
        column_levels(lev)
        masks = level_masks(lev, levels)

        def body(f, carry):
            masks_t = level_masks(levt_ref[...], levels)
            cosine, sine = turn_tables(cs_ref, order_ref[f], masks)
            fields = []
            for i in range(2):
                if slot < 2:
                    cells = [waves_ref[i, p, f, slot * block : (slot + 1) * block] for p in range(2)]
                else:
                    cells = [fast_ref[(i * 2 + p) * freqs + f] for p in range(2)]
                if i == 1:
                    cells[1] = -cells[1]
                fields.append(rotate(cells, cosine, sine))
            store_split(win_ref, (slot, f), inline(lhs_ref[f], fields, masks_t, block))
            return carry

        lax.fori_loop(0, freqs, body, 0)

    for slot in range(2):
        if slot == 0:
            lev = own[half : half + block]
            first, second = 0, 1
        else:
            lev = levw_ref[half : half + block]
            first, second = 1 + c, 2 * (1 - c)
        column_levels(lev)
        masks = level_masks(lev, levels)

        def body(f, carry):
            masks_t = level_masks(levt_ref[...], levels)
            cosine, sine = turn_tables(cs_ref, order_ref[f], masks)
            fields = crossline(lhs_ref[f], win_ref, first, second, f, masks, block)
            if slot == 0:
                img_ref[0, half : half + block] += image_of(fields)
            else:
                acc_ref[...] += image_of(fields)
            fields = [rotate(field, cosine, sine) for field in fields]
            store_split(next_ref, (slot, f), inline(lhs_ref[f], fields, masks_t, block))
            return carry

        lax.fori_loop(0, freqs, body, 0)

    edge_row = pl.multiple_of((rows - half) * (1 - c), half)
    img_ref[0, pl.ds(edge_row, half)] = acc_ref[pl.ds(pl.multiple_of(half * c, half), half)]

    row0 = pl.multiple_of(block * (1 - c), block)
    lev = jnp.where(c == 0, own[block:], own[:block])
    masks = level_masks(lev, levels)
    acc_ref[...] = jnp.zeros_like(acc_ref)

    def body(f, carry):
        fields = crossline(lhs_ref[f], next_ref, c, 1 - c, f, masks, block)
        acc_ref[...] += image_of(fields)
        (sr, si), (qr, qi) = fields
        done_ref[0, 0, f], done_ref[0, 1, f], done_ref[1, 0, f], done_ref[1, 1, f] = sr, si, qr, -qi
        return carry

    lax.fori_loop(0, freqs, body, 0)
    img_ref[1, pl.ds(row0, block)] = acc_ref[...]
    copy = pltpu.make_async_copy(done_ref, out_ref.at[:, :, :, pl.ds(row0, block)], sem)
    copy.start()
    edge_ref[...] = win_ref[c]
    mid_ref[...] = next_ref[0]
    copy.wait()


def second_kernel(
    half_ref, order_ref, cs_ref, slow_ref, lev_ref, lhs_ref, img_in_ref, edge_ref, mid_ref, waves_ref,
    out_ref, img_ref,
    win_ref, next_ref, levw_ref, levt_ref, levu_ref, done_ref, acc_ref, sem,
):
    del waves_ref
    freqs, lhs_rows, _ = lhs_ref.shape
    levels = cs_ref.shape[2]
    block = lhs_rows // (2 * levels)
    half = block // 2
    rows = lev_ref.shape[0]
    c = half_ref[0]
    inside = jnp.where(half_ref[1] == 1, 1.0, 0.0).astype(F32)
    loads = [
        pltpu.make_async_copy(edge_ref, win_ref.at[1 - c], sem.at[0]),
        pltpu.make_async_copy(mid_ref, next_ref.at[1 - c], sem.at[1]),
    ]
    for load in loads:
        load.start()
    own = lev_ref[...].astype(F32)
    slow_plane = slow_ref.shape[0] - 1
    near = jnp.where(c == 0, own[:block], own[block:])
    levw_ref[pl.ds(pl.multiple_of(block * (1 - c), block), block)] = near
    levw_ref[pl.ds(pl.multiple_of(block * c, block), block)] = slow_ref[slow_plane]
    img_ref[...] = img_in_ref[...]
    lev_halo = slow_ref[slow_plane]
    lev_edge = levw_ref[half : half + block]
    levt_ref[...] = to_columns([lev_halo, lev_halo], block)
    levu_ref[...] = to_columns([lev_edge, lev_edge], block)
    masks_halo = level_masks(lev_halo, levels)

    def body(f, carry):
        masks_t = level_masks(levt_ref[...], levels)
        cosine, sine = [inside * t for t in turn_tables(cs_ref, order_ref[f], masks_halo)]
        fields = []
        for i in range(2):
            cells = [slow_ref[(i * 2 + p) * freqs + f] for p in range(2)]
            if i == 1:
                cells[1] = -cells[1]
            fields.append(rotate(cells, cosine, sine))
        store_split(win_ref, (c, f), inline(lhs_ref[f], fields, masks_t, block))
        return carry

    lax.fori_loop(0, freqs, body, 0)
    loads[0].wait()
    loads[1].wait()

    masks_edge = level_masks(lev_edge, levels)
    line = lax.broadcasted_iota(jnp.int32, acc_ref.shape, 0)
    keep = jnp.where((line >= half) == (c == 0), 1.0, inside)
    acc_ref[...] = jnp.zeros_like(acc_ref)

    def body(f, carry):
        masks_t = level_masks(levu_ref[...], levels)
        cosine, sine = [keep * t for t in turn_tables(cs_ref, order_ref[f], masks_edge)]
        fields = crossline(lhs_ref[f], win_ref, 0, 1, f, masks_edge, block)
        acc_ref[...] += image_of(fields)
        fields = [rotate(field, cosine, sine) for field in fields]
        store_split(next_ref, (c, f), inline(lhs_ref[f], fields, masks_t, block))
        return carry

    lax.fori_loop(0, freqs, body, 0)
    edge_row = pl.multiple_of((rows - half) * c, half)
    img_ref[0, pl.ds(edge_row, half)] = acc_ref[pl.ds(pl.multiple_of(half * (1 - c), half), half)]

    masks_near = level_masks(near, levels)
    acc_ref[...] = jnp.zeros_like(acc_ref)

    def body(f, carry):
        fields = crossline(lhs_ref[f], next_ref, 0, 1, f, masks_near, block)
        acc_ref[...] += image_of(fields)
        (sr, si), (qr, qi) = fields
        done_ref[0, 0, f], done_ref[0, 1, f], done_ref[1, 0, f], done_ref[1, 1, f] = sr, si, qr, -qi
        return carry

    lax.fori_loop(0, freqs, body, 0)
    row0 = pl.multiple_of(block * c, block)
    img_ref[1, pl.ds(row0, block)] = acc_ref[...]
    copy = pltpu.make_async_copy(done_ref, out_ref.at[:, :, :, pl.ds(row0, block)], sem.at[0])
    copy.start()
    copy.wait()


VMEM = pl.BlockSpec(memory_space=pltpu.VMEM)
SMEM = pl.BlockSpec(memory_space=pltpu.SMEM)
ANY = pl.BlockSpec(memory_space=pl.ANY)
LIMIT = 48 * 1024 * 1024


def on_device(waves, levels, coeffs, angles, order):
    freqs = order.shape[0]
    rows, width = levels.shape
    level_count, taps = coeffs.shape[2:]
    block = taps - 1
    count = lax.axis_size("strip")
    index = lax.axis_index("strip")
    c = index % 2
    level_plane = levels.astype(F32)[None]

    def boundary(start):
        cells = lax.dynamic_slice_in_dim(waves, start, block, axis=3).reshape(-1, block, width)
        return jnp.concatenate([cells, lax.dynamic_slice_in_dim(level_plane, start, block, axis=1)], axis=0)

    across = [(i, (i + 1) % count if i % 2 else (i - 1) % count) for i in range(count)]
    within = [(i, i + 1 if i % 2 == 0 else i - 1) for i in range(count)]
    slow = lax.ppermute(boundary(c * (rows - block)), "strip", across)
    fast = lax.ppermute(boundary((1 - c) * (rows - block)), "strip", within)

    inside = jnp.where(c == 0, index > 0, index < count - 1)
    where = jnp.stack([c, inside.astype(jnp.int32)]).astype(jnp.int32)
    turns = jnp.stack([jnp.cos(angles), jnp.sin(angles)])
    lhs_shape = (freqs, 2 * level_count * block, 2 * LANES)
    state = (freqs, 2, 2, 2, block, width)
    done = pltpu.VMEM((2, 2, freqs, block, width), F32)
    lane_levels = pltpu.VMEM((LANES, LANES), F32)
    dots = 16 * freqs * 2 * lhs_shape[1] * 192 * width
    out, image, edge, middle, lhs = pl.pallas_call(
        first_kernel,
        out_shape=[
            jax.ShapeDtypeStruct(waves.shape, F32),
            jax.ShapeDtypeStruct((STEPS, rows, width), F32),
            jax.ShapeDtypeStruct(state, BF16),
            jax.ShapeDtypeStruct(state, BF16),
            jax.ShapeDtypeStruct(lhs_shape, BF16),
        ],
        in_specs=[SMEM, SMEM, SMEM, VMEM, VMEM, VMEM, VMEM],
        out_specs=[ANY, VMEM, VMEM, VMEM, VMEM],
        scratch_shapes=[
            pltpu.VMEM(coeffs.shape[:2] + (8, LANES), F32),
            pltpu.VMEM((3,) + state, BF16),
            pltpu.VMEM((2,) + state, BF16),
            pltpu.VMEM((2 * block, width), F32),
            lane_levels,
            done,
            pltpu.VMEM((block, width), F32),
            pltpu.SemaphoreType.DMA,
        ],
        compiler_params=pltpu.CompilerParams(vmem_limit_bytes=LIMIT),
        cost_estimate=pl.CostEstimate(flops=2 * dots, bytes_accessed=8 << 20, transcendentals=0),
        name="own_rows",
    )(where, order, turns, coeffs, waves, levels, fast)
    waves_out, images = pl.pallas_call(
        second_kernel,
        out_shape=[
            jax.ShapeDtypeStruct(waves.shape, F32),
            jax.ShapeDtypeStruct((STEPS, rows, width), F32),
        ],
        in_specs=[SMEM, SMEM, SMEM, VMEM, VMEM, VMEM, VMEM, ANY, ANY, ANY],
        out_specs=[ANY, VMEM],
        scratch_shapes=[
            pltpu.VMEM((2,) + state, BF16),
            pltpu.VMEM((2,) + state, BF16),
            pltpu.VMEM((2 * block, width), F32),
            lane_levels,
            lane_levels,
            done,
            pltpu.VMEM((block, width), F32),
            pltpu.SemaphoreType.DMA((2,)),
        ],
        input_output_aliases={9: 0},
        compiler_params=pltpu.CompilerParams(vmem_limit_bytes=LIMIT),
        cost_estimate=pl.CostEstimate(flops=dots, bytes_accessed=4 << 20, transcendentals=0),
        name="edge_rows",
    )(where, order, turns, slow, levels, lhs, image, edge, middle, out)
    return waves_out, images


def solution(mesh):
    in_specs = (P(None, None, "shot", "strip", None), P("strip", None), P(), P(), P("shot"))
    out_specs = (P(None, None, "shot", "strip", None), P("shot", "strip", None))
    return jax.shard_map(
        on_device, mesh=mesh, in_specs=in_specs, out_specs=out_specs, check_vma=False
    )
```

```python
import functools

import jax
import jax.numpy as jnp
from jax import lax
from jax.experimental import pallas as pl
from jax.experimental.pallas import tpu as pltpu
from jax.sharding import PartitionSpec as P

STEPS = 2
LANES = 128
F32 = jnp.float32
BF16 = jnp.bfloat16


def pick(values, masks):
    out = values[0]
    for value, mask in zip(values[1:], masks):
        out = jnp.where(mask, value, out)
    return out


def level_masks(level, count):
    return [level == float(l) for l in range(1, count)]


def split(cells):
    high = cells.astype(BF16)
    return high, (cells - high.astype(F32)).astype(BF16)


def build_filters(coef_ref, order_ref, pad_ref, lhs_ref, block):
    freqs = lhs_ref.shape[1]
    levels, taps = coef_ref.shape[2:]
    pad_ref[...] = jnp.zeros_like(pad_ref)
    pad_ref[:, :, :levels, :taps] = coef_ref[...]
    wide = 2 * block
    lane = lax.broadcasted_iota(jnp.int32, (block, LANES), 1)
    early = (lane % wide) < block

    def body(f, carry):
        row = order_ref[f]
        real, imag = pad_ref[0, row], pad_ref[1, row]
        tables = (real - pltpu.roll(imag, wide, 1), imag + pltpu.roll(real, wide, 1))
        for level in range(levels):
            for part in range(2):
                line = jnp.broadcast_to(tables[part][level : level + 1], (block, LANES))
                band = pltpu.roll(line, 0, 1, stride=1, stride_axis=0)
                swapped = jnp.where(early, pltpu.roll(band, LANES - block, 1), pltpu.roll(band, block, 1))
                at = (level * 2 + part) * block
                for v, cells in enumerate((band, swapped)):
                    high, low = split(cells)
                    high = high.astype(F32)
                    lhs_ref[v, f, at : at + block, :LANES] = (high + pltpu.roll(high, 2 * wide, 1)).astype(BF16)
                    lhs_ref[v, f, at : at + block, LANES:] = low
        return carry

    lax.fori_loop(0, freqs, body, 0)


def band_product(lhs, reals, imags):
    rhs = jnp.concatenate([reals[0], imags[0], reals[1], imags[1], reals[0], imags[0]], axis=0)
    return jnp.dot(lhs[:, : rhs.shape[0]], rhs, preferred_element_type=F32)


def band_pick(found, masks, block):
    count = found.shape[0] // (2 * block)
    return [
        pick([found[(l * 2 + part) * block : (l * 2 + part + 1) * block] for l in range(count)], masks)
        for part in range(2)
    ]


def turn_tables(turn_ref, f, masks):
    height, width = masks[0].shape
    tables = []
    for part in range(2):
        values = []
        for l in range(len(masks) + 1):
            tile = turn_ref[f, part, l]
            tile = jnp.concatenate([tile] * (height // tile.shape[0]), axis=0)
            values.append(jnp.concatenate([tile] * (width // LANES), axis=1))
        tables.append(pick(values, masks))
    return tables


def rotate(cells, cosine, sine):
    real, imag = cells
    return real * cosine - imag * sine, real * sine + imag * cosine


def to_columns(fields, block):
    chunks = fields[0].shape[1] // LANES
    return jnp.concatenate(
        [field[:, c * LANES : (c + 1) * LANES] for c in range(chunks) for field in fields], axis=0
    ).T


def inline(lhs, fields, masks_t, block):
    half = block // 2
    count = len(fields)
    chunks = fields[0][0].shape[1] // LANES
    step = count * block
    lane = lax.broadcasted_iota(jnp.int32, (half, LANES), 1)
    columns = []
    for part in range(2):
        columns.append(to_columns([field[part] for field in fields], block))
        yield
    parts = []
    for cols in columns:
        before = jnp.where(lane < step, 0.0, pltpu.roll(cols[LANES - half :], step, 1))
        after = jnp.where(lane >= LANES - step, 0.0, pltpu.roll(cols[:half], LANES - step, 1))
        parts.append(split(jnp.concatenate([before, cols, after], axis=0)))
        yield
    mid = LANES // 2
    halves = [[[], []], [[], []]]
    masks_t = masks_t()
    found = []
    spots = list(range(0, mid, block))

    def finish(at):
        masks = [jnp.concatenate([m[at : at + block], m[mid + at : mid + at + block]], axis=1) for m in masks_t]
        got = band_pick(found.pop(0), masks, block)
        for part in range(2):
            halves[part][0].append(got[part][:, :LANES])
            halves[part][1].append(got[part][:, LANES:])

    for n, at in enumerate(spots):
        windows = [
            [
                jnp.concatenate([x[at : at + 2 * block], x[mid + at : mid + at + 2 * block]], axis=1)
                for x in parts[part]
            ]
            for part in range(2)
        ]
        found.append(band_product(lhs, windows[0], windows[1]))
        yield
        if n >= LAG:
            finish(spots[n - LAG])
    for at in spots[len(spots) - LAG :]:
        finish(at)
    yield
    back = []
    for part in range(2):
        back.append(jnp.concatenate(halves[part][0] + halves[part][1], axis=0).T)
        yield
    return [
        [
            jnp.concatenate(
                [back[part][(c * count + i) * block : (c * count + i + 1) * block] for c in range(chunks)], axis=1
            )
            for part in range(2)
        ]
        for i in range(count)
    ]


def split_fields(fields):
    return [list(zip(*[split(cells) for cells in field])) for field in fields]


def saved(ref, f):
    return [[[ref[f, i, kind, part] for part in range(2)] for kind in range(2)] for i in range(2)]


def save(ref, f, blocks):
    for i in range(2):
        for kind in range(2):
            for part in range(2):
                ref[f, i, kind, part] = blocks[i][kind][part]


def crossline(lhs, first, second, masks, block):
    wide = 2 * LANES
    width = first[0][0][0].shape[1]
    pieces = [[[], []], [[], []]]
    spots = [(i, at) for i in range(2) for at in range(0, width, wide)]
    found = []

    def finish(spot):
        i, at = spot
        got = band_pick(found.pop(0), [m[:, at : at + wide] for m in masks], block)
        for part in range(2):
            pieces[i][part].append(got[part])

    for n, (i, at) in enumerate(spots):
        windows = [
            [
                jnp.concatenate([b[i][kind][part][:, at : at + wide] for b in (first, second)], axis=0)
                for kind in range(2)
            ]
            for part in range(2)
        ]
        found.append(band_product(lhs, windows[0], windows[1]))
        yield
        if n >= LAG:
            finish(spots[n - LAG])
    for spot in spots[len(spots) - LAG :]:
        finish(spot)
    yield
    return [[jnp.concatenate(p, axis=1) for p in piece] for piece in pieces]


def interleave(chains, skew):
    live = dict(enumerate(chains))
    tick = 0
    while live:
        for n in list(live):
            if tick >= n * skew and next(live[n], live) is live:
                del live[n]
        tick += 1


def image_of(fields):
    (sr, si), (qr, qi) = fields
    return sr * qr - si * qi


def raw_fields(get, cosine, sine):
    fields = [[get(i, p) for p in range(2)] for i in range(2)]
    fields[1][1] = -fields[1][1]
    return [rotate(field, cosine, sine) for field in fields]


def put_done(done_ref, f, fields):
    (sr, si), (qr, qi) = fields
    done_ref[0, 0, f], done_ref[0, 1, f], done_ref[1, 0, f], done_ref[1, 1, f] = sr, si, qr, -qi


def window_levels(ref, inner, outer, inner_at, block):
    ref[pl.ds(pl.multiple_of(inner_at, block), block)] = inner
    ref[pl.ds(pl.multiple_of(block - inner_at, block), block)] = outer
    return ref[block // 2 : block // 2 + block]


def first_kernel(
    order_ref, cs_ref, coef_ref, waves_ref, lev_ref, fast_ref, halo_ref,
    out_ref, img_ref, edge_ref, mid_ref, lhs_ref, turn_ref,
    pad_ref, levw_ref, levt_ref, done_ref, acc_ref, sem,
):
    freqs = lhs_ref.shape[1]
    levels, taps = coef_ref.shape[2:]
    block = taps - 1
    half = block // 2
    rows = lev_ref.shape[0]
    c = lax.axis_index("strip") % 2
    for f in range(freqs):
        for part in range(2):
            for l in range(levels):
                turn_ref[f, part, l] = jnp.full(turn_ref.shape[3:], cs_ref[part, order_ref[f], l], F32)
    build_filters(coef_ref, order_ref, pad_ref, lhs_ref, block)
    slow_row = pl.multiple_of(block * c, block)
    fast_row = pl.multiple_of(block * (1 - c), block)
    lev_slow = lev_ref[pl.ds(slow_row, block)].astype(F32)
    lev_fast = lev_ref[pl.ds(fast_row, block)].astype(F32)
    lev_halo = halo_ref[...].astype(F32)
    lev_mid = lev_ref[half : half + block].astype(F32)
    lev_edge = window_levels(levw_ref, lev_fast, lev_halo, block * c, block)
    blocks = (lev_slow, lev_fast, lev_halo, lev_mid, lev_edge)
    for slot, lev in enumerate(blocks):
        levt_ref[slot] = to_columns([lev, lev], block)
    masks = [level_masks(lev, levels) for lev in blocks]
    acc_ref[...] = jnp.zeros_like(acc_ref)
    copies = []
    ready = {}

    def start_chain(f, slot):
        cosine, sine = turn_tables(turn_ref, f, masks[slot])
        if slot < 2:
            at = (slow_row, fast_row)[slot]
            get = lambda i, p: waves_ref[i, p, f, pl.ds(at, block)]
        else:
            get = lambda i, p: fast_ref[(i * 2 + p) * freqs + f]
        fields = raw_fields(get, cosine, sine)
        yield
        fields = yield from inline(lhs_ref[0, f], fields, lambda: level_masks(levt_ref[slot], levels), block)
        ready[f, slot] = split_fields(fields)
        if slot == 0:
            save(edge_ref, f, ready[f, slot])

    def next_chain(f, slot):
        first, second = ((0, 1), (1, 2))[slot]
        fields = yield from crossline(lhs_ref[c, f], ready[f, first], ready[f, second], masks[3 + slot], block)
        acc_ref[slot] += image_of(fields)
        cosine, sine = turn_tables(turn_ref, f, masks[3 + slot])
        fields = [rotate(field, cosine, sine) for field in fields]
        yield
        fields = yield from inline(lhs_ref[0, f], fields, lambda: level_masks(levt_ref[3 + slot], levels), block)
        ready[f, 3 + slot] = split_fields(fields)
        if slot == 0:
            save(mid_ref, f, ready[f, 3])

    def last_chain(f):
        fields = yield from crossline(lhs_ref[c, f], ready[f, 3], ready[f, 4], masks[1], block)
        acc_ref[2] += image_of(fields)
        put_done(done_ref, f, fields)
        copies.append(
            pltpu.make_async_copy(done_ref.at[:, :, f], out_ref.at[:, :, f, pl.ds(fast_row, block)], sem.at[f])
        )
        copies[-1].start()

    interleave([start_chain(f, slot) for f in range(freqs) for slot in range(3)], SKEW1)
    interleave([next_chain(f, slot) for f in range(freqs) for slot in range(2)], SKEW1)
    copies.append(pltpu.make_async_copy(acc_ref.at[0], img_ref.at[0, pl.ds(half, block)], sem.at[freqs]))
    own_row = pl.multiple_of(half * c, half)
    edge_row = pl.multiple_of((rows - half) * (1 - c), half)
    copies.append(
        pltpu.make_async_copy(
            acc_ref.at[1, pl.ds(own_row, half)], img_ref.at[0, pl.ds(edge_row, half)], sem.at[freqs + 1]
        )
    )
    for copy in copies:
        copy.start()
    interleave([last_chain(f) for f in range(freqs)], SKEW1)
    copies.append(pltpu.make_async_copy(acc_ref.at[2], img_ref.at[1, pl.ds(fast_row, block)], sem.at[freqs + 2]))
    copies[-1].start()
    for copy in copies:
        copy.wait()


def second_kernel(
    offset, first, last,
    slow_ref, halo_ref, lev_ref, lhs_ref, turn_ref, edge_ref, mid_ref, *refs,
):
    if first:
        sum_in_ref = None
        waves_ref, img_in_ref, out_ref, img_ref, sum_ref, levw_ref, levt_ref, done_ref, sem = refs
    else:
        sum_in_ref, waves_ref, img_in_ref, out_ref, img_ref, sum_ref, levw_ref, levt_ref, done_ref, sem = refs
    del img_in_ref
    del waves_ref
    levels = turn_ref.shape[2]
    block = lhs_ref.shape[2] // (2 * levels)
    group = done_ref.shape[2]
    half = block // 2
    rows = lev_ref.shape[0]
    index = lax.axis_index("strip")
    c = index % 2
    outside = jnp.where(c == 0, index == 0, index == lax.axis_size("strip") - 1)
    inside = jnp.where(outside, 0.0, 1.0).astype(F32)
    slow_row = pl.multiple_of(block * c, block)
    lev_near = lev_ref[pl.ds(slow_row, block)].astype(F32)
    lev_halo = halo_ref[...].astype(F32)
    lev_edge = window_levels(levw_ref, lev_near, lev_halo, block * (1 - c), block)
    for slot, lev in enumerate((lev_halo, lev_edge)):
        levt_ref[slot] = to_columns([lev, lev], block)
    masks_near, masks_halo, masks_edge = [level_masks(lev, levels) for lev in (lev_near, lev_halo, lev_edge)]
    line = lax.broadcasted_iota(jnp.int32, lev_edge.shape, 0)
    keep = jnp.where((line >= half) == (c == 0), 1.0, inside)
    sum_ref[...] = jnp.zeros_like(sum_ref) if first else sum_in_ref[...]
    copies = []

    def chain(g):
        f = offset + g
        cosine, sine = [inside * t for t in turn_tables(turn_ref, f, masks_halo)]
        get = lambda i, p: slow_ref[(i * 2 + p) * group + g]
        fields = raw_fields(get, cosine, sine)
        yield
        fields = yield from inline(lhs_ref[0, f], fields, lambda: level_masks(levt_ref[0], levels), block)
        outer = split_fields(fields)
        yield
        fields = yield from crossline(lhs_ref[1 - c, f], saved(edge_ref, f), outer, masks_edge, block)
        sum_ref[0] += image_of(fields)
        cosine, sine = [keep * t for t in turn_tables(turn_ref, f, masks_edge)]
        fields = [rotate(field, cosine, sine) for field in fields]
        yield
        if last and g == group - 1:
            own_row = pl.multiple_of(half * (1 - c), half)
            edge_row = pl.multiple_of((rows - half) * c, half)
            copies.append(
                pltpu.make_async_copy(
                    sum_ref.at[0, pl.ds(own_row, half)], img_ref.at[0, pl.ds(edge_row, half)], sem.at[group]
                )
            )
            copies[-1].start()
        fields = yield from inline(lhs_ref[0, f], fields, lambda: level_masks(levt_ref[1], levels), block)
        outer = split_fields(fields)
        yield
        fields = yield from crossline(lhs_ref[1 - c, f], saved(mid_ref, f), outer, masks_near, block)
        sum_ref[1] += image_of(fields)
        put_done(done_ref, g, fields)
        copies.append(
            pltpu.make_async_copy(done_ref.at[:, :, g], out_ref.at[:, :, f, pl.ds(slow_row, block)], sem.at[g])
        )
        copies[-1].start()

    interleave([chain(g) for g in range(group)], SKEW)
    if last:
        copies.append(
            pltpu.make_async_copy(sum_ref.at[1], img_ref.at[1, pl.ds(slow_row, block)], sem.at[group + 1])
        )
        copies[-1].start()
    for copy in copies:
        copy.wait()


VMEM = pl.BlockSpec(memory_space=pltpu.VMEM)
SMEM = pl.BlockSpec(memory_space=pltpu.SMEM)
ANY = pl.BlockSpec(memory_space=pl.ANY)
LIMIT = 48 * 1024 * 1024
SKEW = 3
SKEW1 = 2
LAG = 1
GROUPS = 1


def on_device(waves, levels, coeffs, angles, order):
    freqs = order.shape[0]
    rows, width = levels.shape
    level_count, taps = coeffs.shape[2:]
    block = taps - 1
    count = lax.axis_size("strip")
    index = lax.axis_index("strip")
    c = index % 2
    groups = GROUPS if freqs % GROUPS == 0 else 1
    group = freqs // groups

    def side(cells, start, low=0, high=freqs):
        cells = lax.dynamic_slice_in_dim(cells, start, block, axis=3)
        return cells[:, :, low:high].reshape(-1, block, width)

    shots = lax.axis_size("shot")
    across, within = [], []
    for shot in range(shots):
        for i in range(count):
            j = i + 1 if i % 2 else i - 1
            other = shot if 0 <= j < count else min(shot ^ 1, shots - 1)
            across.append((shot * count + i, other * count + (j if 0 <= j < count else i)))
            within.append((shot * count + i, shot * count + (i ^ 1)))
    axes = ("shot", "strip")

    slow_row, fast_row = c * (rows - block), (1 - c) * (rows - block)
    slow = [lax.ppermute(side(waves, slow_row, 0, group), axes, across)]
    fast = lax.ppermute(side(waves, fast_row), axes, within)
    cells, marks, fast = lax.optimization_barrier((waves, levels, fast))
    fast_levels = lax.ppermute(lax.dynamic_slice_in_dim(marks, fast_row, block, axis=0), axes, within)
    slow_levels = lax.ppermute(lax.dynamic_slice_in_dim(marks, slow_row, block, axis=0), axes, across)
    for g in range(1, groups):
        slow.append(lax.ppermute(side(cells, slow_row, g * group, (g + 1) * group), axes, across))

    turns = jnp.stack([jnp.cos(angles), jnp.sin(angles)])
    lhs_shape = (2, freqs, 2 * level_count * block, 2 * LANES)
    state = (freqs, 2, 2, 2, block, width)
    dots = 16 * freqs * 2 * lhs_shape[2] * 12 * block * width
    waves_out, image, edge, middle, lhs, tiles = pl.pallas_call(
        first_kernel,
        out_shape=[
            jax.ShapeDtypeStruct(waves.shape, F32),
            jax.ShapeDtypeStruct((STEPS, rows, width), F32),
            jax.ShapeDtypeStruct(state, BF16),
            jax.ShapeDtypeStruct(state, BF16),
            jax.ShapeDtypeStruct(lhs_shape, BF16),
            jax.ShapeDtypeStruct((freqs, 2, level_count, 8, LANES), F32),
        ],
        in_specs=[SMEM, SMEM, VMEM, VMEM, VMEM, VMEM, VMEM],
        out_specs=[ANY, ANY, VMEM, VMEM, VMEM, VMEM],
        scratch_shapes=[
            pltpu.VMEM(coeffs.shape[:2] + (8, LANES), F32),
            pltpu.VMEM((2 * block, width), F32),
            pltpu.VMEM((5, LANES, LANES), F32),
            pltpu.VMEM((2, 2, freqs, block, width), F32),
            pltpu.VMEM((3, block, width), F32),
            pltpu.SemaphoreType.DMA((freqs + 3,)),
        ],
        compiler_params=pltpu.CompilerParams(vmem_limit_bytes=LIMIT),
        cost_estimate=pl.CostEstimate(flops=2 * dots, bytes_accessed=8 << 20, transcendentals=0),
        name="own_rows",
    )(order, turns, coeffs, waves, levels, fast, fast_levels)
    total = []
    for g in range(groups):
        aliased = 7 + len(total)
        waves_out, image, *total = pl.pallas_call(
            functools.partial(second_kernel, g * group, g == 0, g == groups - 1),
            out_shape=[
                jax.ShapeDtypeStruct(waves.shape, F32),
                jax.ShapeDtypeStruct((STEPS, rows, width), F32),
                jax.ShapeDtypeStruct((STEPS, block, width), F32),
            ],
            in_specs=[VMEM] * aliased + [ANY, ANY],
            out_specs=[ANY, ANY, VMEM],
            scratch_shapes=[
                pltpu.VMEM((2 * block, width), F32),
                pltpu.VMEM((2, LANES, LANES), F32),
                pltpu.VMEM((2, 2, group, block, width), F32),
                pltpu.SemaphoreType.DMA((group + 2,)),
            ],
            input_output_aliases={aliased: 0, aliased + 1: 1},
            compiler_params=pltpu.CompilerParams(vmem_limit_bytes=LIMIT),
            cost_estimate=pl.CostEstimate(flops=dots // groups, bytes_accessed=4 << 20, transcendentals=0),
            name=f"edge_rows_{g}",
        )(slow[g], slow_levels, levels, lhs, tiles, edge, middle, *total, waves_out, image)
    return waves_out, image


def solution(mesh):
    in_specs = (P(None, None, "shot", "strip", None), P("strip", None), P(), P(), P("shot"))
    out_specs = (P(None, None, "shot", "strip", None), P("shot", "strip", None))
    return jax.shard_map(
        on_device, mesh=mesh, in_specs=in_specs, out_specs=out_specs, check_vma=False
    )
```

```python
import functools

import jax
import jax.numpy as jnp
from jax import lax
from jax.experimental import pallas as pl
from jax.experimental.pallas import tpu as pltpu
from jax.sharding import PartitionSpec as P

STEPS = 2
LANES = 128
F32 = jnp.float32
BF16 = jnp.bfloat16


def pick(values, masks):
    out = values[0]
    for value, mask in zip(values[1:], masks):
        out = jnp.where(mask, value, out)
    return out


def level_masks(level, count):
    return [level == float(l) for l in range(1, count)]


def split(cells):
    high = cells.astype(BF16)
    return high, (cells - high.astype(F32)).astype(BF16)


def build_filters(coef_ref, order_ref, pad_ref, lhs_ref, block):
    freqs = lhs_ref.shape[1]
    levels, taps = coef_ref.shape[2:]
    pad_ref[...] = jnp.zeros_like(pad_ref)
    pad_ref[:, :, :levels, :taps] = coef_ref[...]
    wide = 2 * block
    lane = lax.broadcasted_iota(jnp.int32, (block, LANES), 1)
    early = (lane % wide) < block

    def body(f, carry):
        row = order_ref[f]
        real, imag = pad_ref[0, row], pad_ref[1, row]
        tables = (real - pltpu.roll(imag, wide, 1), imag + pltpu.roll(real, wide, 1))
        for level in range(levels):
            for part in range(2):
                line = jnp.broadcast_to(tables[part][level : level + 1], (block, LANES))
                band = pltpu.roll(line, 0, 1, stride=1, stride_axis=0)
                swapped = jnp.where(early, pltpu.roll(band, LANES - block, 1), pltpu.roll(band, block, 1))
                at = (level * 2 + part) * block
                for v, cells in enumerate((band, swapped)):
                    high, low = split(cells)
                    high = high.astype(F32)
                    lhs_ref[v, f, at : at + block, :LANES] = (high + pltpu.roll(high, 2 * wide, 1)).astype(BF16)
                    lhs_ref[v, f, at : at + block, LANES:] = low
        return carry

    for f in range(freqs):
        body(f, 0)


def band_product(lhs, reals, imags):
    rhs = jnp.concatenate([reals[0], imags[0], reals[1], imags[1], reals[0], imags[0]], axis=0)
    return jnp.dot(lhs[:, : rhs.shape[0]], rhs, preferred_element_type=F32)


def band_pick(found, masks, block):
    count = found.shape[0] // (2 * block)
    return [
        pick([found[(l * 2 + part) * block : (l * 2 + part + 1) * block] for l in range(count)], masks)
        for part in range(2)
    ]


def turn_tables(turn_ref, f, masks):
    height, width = masks[0].shape
    tables = []
    for part in range(2):
        values = []
        for l in range(len(masks) + 1):
            tile = turn_ref[f, part, l]
            tile = jnp.concatenate([tile] * (height // tile.shape[0]), axis=0)
            values.append(jnp.concatenate([tile] * (width // LANES), axis=1))
        tables.append(pick(values, masks))
    return tables


def rotate(cells, cosine, sine):
    real, imag = cells
    return real * cosine - imag * sine, real * sine + imag * cosine


def to_columns(fields, block):
    chunks = fields[0].shape[1] // LANES
    return jnp.concatenate(
        [field[:, c * LANES : (c + 1) * LANES] for c in range(chunks) for field in fields], axis=0
    ).T


def inline(lhs, fields, masks_t, block):
    half = block // 2
    count = len(fields)
    chunks = fields[0][0].shape[1] // LANES
    step = count * block
    lane = lax.broadcasted_iota(jnp.int32, (half, LANES), 1)
    columns = []
    for part in range(2):
        columns.append(to_columns([field[part] for field in fields], block))
        yield
    parts = []
    for cols in columns:
        before = jnp.where(lane < step, 0.0, pltpu.roll(cols[LANES - half :], step, 1))
        after = jnp.where(lane >= LANES - step, 0.0, pltpu.roll(cols[:half], LANES - step, 1))
        parts.append(split(jnp.concatenate([before, cols, after], axis=0)))
        yield
    mid = LANES // 2
    halves = [[[], []], [[], []]]
    masks_t = masks_t()
    found = []
    spots = list(range(0, mid, block))

    def finish(at):
        masks = [jnp.concatenate([m[at : at + block], m[mid + at : mid + at + block]], axis=1) for m in masks_t]
        got = band_pick(found.pop(0), masks, block)
        for part in range(2):
            halves[part][0].append(got[part][:, :LANES])
            halves[part][1].append(got[part][:, LANES:])

    for n, at in enumerate(spots):
        windows = [
            [
                jnp.concatenate([x[at : at + 2 * block], x[mid + at : mid + at + 2 * block]], axis=1)
                for x in parts[part]
            ]
            for part in range(2)
        ]
        found.append(band_product(lhs, windows[0], windows[1]))
        yield
        if n >= LAG:
            finish(spots[n - LAG])
    for at in spots[len(spots) - LAG :]:
        finish(at)
    yield
    back = []
    for part in range(2):
        back.append(jnp.concatenate(halves[part][0] + halves[part][1], axis=0).T)
        yield
    return [
        [
            jnp.concatenate(
                [back[part][(c * count + i) * block : (c * count + i + 1) * block] for c in range(chunks)], axis=1
            )
            for part in range(2)
        ]
        for i in range(count)
    ]


def split_fields(fields):
    return [list(zip(*[split(cells) for cells in field])) for field in fields]


def saved(ref, f):
    return [[[ref[f, i, kind, part] for part in range(2)] for kind in range(2)] for i in range(2)]


def save(ref, f, blocks):
    for i in range(2):
        for kind in range(2):
            for part in range(2):
                ref[f, i, kind, part] = blocks[i][kind][part]


def crossline(lhs, first, second, masks, block):
    wide = 2 * LANES
    width = first[0][0][0].shape[1]
    pieces = [[[], []], [[], []]]
    spots = [(i, at) for i in range(2) for at in range(0, width, wide)]
    found = []

    def finish(spot):
        i, at = spot
        got = band_pick(found.pop(0), [m[:, at : at + wide] for m in masks], block)
        for part in range(2):
            pieces[i][part].append(got[part])

    for n, (i, at) in enumerate(spots):
        windows = [
            [
                jnp.concatenate([b[i][kind][part][:, at : at + wide] for b in (first, second)], axis=0)
                for kind in range(2)
            ]
            for part in range(2)
        ]
        found.append(band_product(lhs, windows[0], windows[1]))
        yield
        if n >= LAG:
            finish(spots[n - LAG])
    for spot in spots[len(spots) - LAG :]:
        finish(spot)
    yield
    return [[jnp.concatenate(p, axis=1) for p in piece] for piece in pieces]


def interleave(chains, skew):
    live = dict(enumerate(chains))
    tick = 0
    while live:
        for n in list(live):
            if tick >= n * skew and next(live[n], live) is live:
                del live[n]
        tick += 1


def image_of(fields):
    (sr, si), (qr, qi) = fields
    return sr * qr - si * qi


def raw_fields(get, cosine, sine):
    fields = [[get(i, p) for p in range(2)] for i in range(2)]
    fields[1][1] = -fields[1][1]
    return [rotate(field, cosine, sine) for field in fields]


def put_done(done_ref, f, fields):
    (sr, si), (qr, qi) = fields
    done_ref[0, 0, f], done_ref[0, 1, f], done_ref[1, 0, f], done_ref[1, 1, f] = sr, si, qr, -qi


def window_levels(ref, inner, outer, inner_at, block):
    ref[pl.ds(pl.multiple_of(inner_at, block), block)] = inner
    ref[pl.ds(pl.multiple_of(block - inner_at, block), block)] = outer
    return ref[block // 2 : block // 2 + block]


def first_kernel(
    order_ref, cs_ref, coef_ref, waves_ref, lev_ref, fast_ref, halo_ref,
    done_ref, acc_ref, edge_ref, mid_ref, lhs_ref, turn_ref,
    pad_ref, levw_ref, levt_ref,
):
    freqs = lhs_ref.shape[1]
    levels, taps = coef_ref.shape[2:]
    block = taps - 1
    half = block // 2
    c = lax.axis_index("strip") % 2
    for f in range(freqs):
        for part in range(2):
            for l in range(levels):
                turn_ref[f, part, l] = jnp.full(turn_ref.shape[3:], cs_ref[part, order_ref[f], l], F32)
    build_filters(coef_ref, order_ref, pad_ref, lhs_ref, block)
    slow_row = pl.multiple_of(block * c, block)
    fast_row = pl.multiple_of(block * (1 - c), block)
    lev_slow = lev_ref[pl.ds(slow_row, block)].astype(F32)
    lev_fast = lev_ref[pl.ds(fast_row, block)].astype(F32)
    lev_halo = halo_ref[...].astype(F32)
    lev_mid = lev_ref[half : half + block].astype(F32)
    lev_edge = window_levels(levw_ref, lev_fast, lev_halo, block * c, block)
    blocks = (lev_slow, lev_fast, lev_halo, lev_mid, lev_edge)
    for slot, lev in enumerate(blocks):
        levt_ref[slot] = to_columns([lev, lev], block)
    masks = [level_masks(lev, levels) for lev in blocks]
    acc_ref[...] = jnp.zeros_like(acc_ref)
    ready = {}

    def start_chain(f, slot):
        cosine, sine = turn_tables(turn_ref, f, masks[slot])
        if slot < 2:
            at = (slow_row, fast_row)[slot]
            get = lambda i, p: waves_ref[i, p, f, pl.ds(at, block)]
        else:
            get = lambda i, p: fast_ref[(i * 2 + p) * freqs + f]
        fields = raw_fields(get, cosine, sine)
        yield
        fields = yield from inline(lhs_ref[0, f], fields, lambda: level_masks(levt_ref[slot], levels), block)
        ready[f, slot] = split_fields(fields)
        if slot == 0:
            save(edge_ref, f, ready[f, slot])

    def next_chain(f, slot):
        first, second = ((0, 1), (1, 2))[slot]
        fields = yield from crossline(lhs_ref[c, f], ready[f, first], ready[f, second], masks[3 + slot], block)
        acc_ref[slot] += image_of(fields)
        cosine, sine = turn_tables(turn_ref, f, masks[3 + slot])
        fields = [rotate(field, cosine, sine) for field in fields]
        yield
        fields = yield from inline(lhs_ref[0, f], fields, lambda: level_masks(levt_ref[3 + slot], levels), block)
        ready[f, 3 + slot] = split_fields(fields)
        if slot == 0:
            save(mid_ref, f, ready[f, 3])

    def last_chain(f):
        fields = yield from crossline(lhs_ref[c, f], ready[f, 3], ready[f, 4], masks[1], block)
        acc_ref[2] += image_of(fields)
        put_done(done_ref, f, fields)

    interleave([start_chain(f, slot) for f in range(freqs) for slot in range(3)], SKEW1)
    interleave([next_chain(f, slot) for f in range(freqs) for slot in range(2)], SKEW1)
    interleave([last_chain(f) for f in range(freqs)], SKEW1)


def second_kernel(
    offset, first, last,
    slow_ref, halo_ref, lev_ref, lhs_ref, turn_ref, edge_ref, mid_ref, *refs,
):
    refs = list(refs)
    sum_in_ref = None if first else refs.pop(0)
    if last:
        out_ref, img_ref, sum_ref, done_ref, levw_ref, levt_ref, sem = refs[-7:]
        own_ref, own_sum_ref, *before = refs[:-7]
    else:
        sum_ref, done_ref, levw_ref, levt_ref = refs
    levels = turn_ref.shape[2]
    block = lhs_ref.shape[2] // (2 * levels)
    group = done_ref.shape[2]
    half = block // 2
    rows = lev_ref.shape[0]
    index = lax.axis_index("strip")
    c = index % 2
    outside = jnp.where(c == 0, index == 0, index == lax.axis_size("strip") - 1)
    inside = jnp.where(outside, 0.0, 1.0).astype(F32)
    slow_row = pl.multiple_of(block * c, block)
    lev_near = lev_ref[pl.ds(slow_row, block)].astype(F32)
    lev_halo = halo_ref[...].astype(F32)
    lev_edge = window_levels(levw_ref, lev_near, lev_halo, block * (1 - c), block)
    for slot, lev in enumerate((lev_halo, lev_edge)):
        levt_ref[slot] = to_columns([lev, lev], block)
    masks_near, masks_halo, masks_edge = [level_masks(lev, levels) for lev in (lev_near, lev_halo, lev_edge)]
    line = lax.broadcasted_iota(jnp.int32, lev_edge.shape, 0)
    keep = jnp.where((line >= half) == (c == 0), 1.0, inside)
    sum_ref[...] = jnp.zeros_like(sum_ref) if first else sum_in_ref[...]
    copies = []

    def send(source, target):
        copies.append(pltpu.make_async_copy(source, target, sem.at[len(copies)]))
        copies[-1].start()

    if last:
        fast_row = pl.multiple_of(block * (1 - c), block)
        own_half = pl.ds(pl.multiple_of(half * c, half), half)
        own_edge = pl.ds(pl.multiple_of((rows - half) * (1 - c), half), half)
        send(own_ref, out_ref.at[:, :, :, pl.ds(fast_row, block)])
        for n, ref in enumerate(before):
            send(ref, out_ref.at[:, :, pl.ds(n * group, group), pl.ds(slow_row, block)])
        send(own_sum_ref.at[0], img_ref.at[0, pl.ds(half, block)])
        send(own_sum_ref.at[1, own_half], img_ref.at[0, own_edge])
        send(own_sum_ref.at[2], img_ref.at[1, pl.ds(fast_row, block)])

    def chain(g):
        f = offset + g
        cosine, sine = [inside * t for t in turn_tables(turn_ref, f, masks_halo)]
        get = lambda i, p: slow_ref[(i * 2 + p) * group + g]
        fields = raw_fields(get, cosine, sine)
        yield
        fields = yield from inline(lhs_ref[0, f], fields, lambda: level_masks(levt_ref[0], levels), block)
        outer = split_fields(fields)
        yield
        fields = yield from crossline(lhs_ref[1 - c, f], saved(edge_ref, f), outer, masks_edge, block)
        sum_ref[0] += image_of(fields)
        cosine, sine = [keep * t for t in turn_tables(turn_ref, f, masks_edge)]
        fields = [rotate(field, cosine, sine) for field in fields]
        yield
        if last and g == group - 1:
            own_row = pl.multiple_of(half * (1 - c), half)
            edge_row = pl.multiple_of((rows - half) * c, half)
            send(sum_ref.at[0, pl.ds(own_row, half)], img_ref.at[0, pl.ds(edge_row, half)])
        fields = yield from inline(lhs_ref[0, f], fields, lambda: level_masks(levt_ref[1], levels), block)
        outer = split_fields(fields)
        yield
        fields = yield from crossline(lhs_ref[1 - c, f], saved(mid_ref, f), outer, masks_near, block)
        sum_ref[1] += image_of(fields)
        put_done(done_ref, g, fields)
        if last:
            send(done_ref.at[:, :, g], out_ref.at[:, :, f, pl.ds(slow_row, block)])

    interleave([chain(g) for g in range(group)], SKEW)
    if last:
        send(sum_ref.at[1], img_ref.at[1, pl.ds(slow_row, block)])
    for copy in copies:
        copy.wait()


VMEM = pl.BlockSpec(memory_space=pltpu.VMEM)
SMEM = pl.BlockSpec(memory_space=pltpu.SMEM)
ANY = pl.BlockSpec(memory_space=pl.ANY)
LIMIT = 48 * 1024 * 1024
SKEW = 3
SKEW1 = 2
LAG = 1
GROUPS = 2


def on_device(waves, levels, coeffs, angles, order):
    freqs = order.shape[0]
    rows, width = levels.shape
    level_count, taps = coeffs.shape[2:]
    block = taps - 1
    count = lax.axis_size("strip")
    index = lax.axis_index("strip")
    c = index % 2
    groups = GROUPS if freqs % GROUPS == 0 else 1
    group = freqs // groups

    def side(cells, start, low=0, high=freqs):
        cells = lax.dynamic_slice_in_dim(cells, start, block, axis=3)
        return cells[:, :, low:high].reshape(-1, block, width)

    shots = lax.axis_size("shot")
    across, within = [], []
    for shot in range(shots):
        for i in range(count):
            j = i + 1 if i % 2 else i - 1
            other = shot if 0 <= j < count else min(shot ^ 1, shots - 1)
            across.append((shot * count + i, other * count + (j if 0 <= j < count else i)))
            within.append((shot * count + i, shot * count + (i ^ 1)))
    axes = ("shot", "strip")

    slow_row, fast_row = c * (rows - block), (1 - c) * (rows - block)
    slow = [lax.ppermute(side(waves, slow_row, 0, group), axes, across)]
    near = side(waves, fast_row)
    fast = lax.ppermute(near, axes, within)
    cells, marks, _ = lax.optimization_barrier((waves, levels, near))
    fast_levels = lax.ppermute(lax.dynamic_slice_in_dim(marks, fast_row, block, axis=0), axes, within)
    slow_levels = lax.ppermute(lax.dynamic_slice_in_dim(marks, slow_row, block, axis=0), axes, across)
    for g in range(1, groups):
        slow.append(lax.ppermute(side(cells, slow_row, g * group, (g + 1) * group), axes, across))

    turns = jnp.stack([jnp.cos(angles), jnp.sin(angles)])
    lhs_shape = (2, freqs, 2 * level_count * block, 2 * LANES)
    state = (freqs, 2, 2, 2, block, width)
    dots = 16 * freqs * 2 * lhs_shape[2] * 12 * block * width
    own_done, own_sum, edge, middle, lhs, tiles = pl.pallas_call(
        first_kernel,
        out_shape=[
            jax.ShapeDtypeStruct((2, 2, freqs, block, width), F32),
            jax.ShapeDtypeStruct((3, block, width), F32),
            jax.ShapeDtypeStruct(state, BF16),
            jax.ShapeDtypeStruct(state, BF16),
            jax.ShapeDtypeStruct(lhs_shape, BF16),
            jax.ShapeDtypeStruct((freqs, 2, level_count, 8, LANES), F32),
        ],
        in_specs=[SMEM, SMEM, VMEM, VMEM, VMEM, VMEM, VMEM],
        out_specs=[VMEM] * 6,
        scratch_shapes=[
            pltpu.VMEM(coeffs.shape[:2] + (8, LANES), F32),
            pltpu.VMEM((2 * block, width), F32),
            pltpu.VMEM((5, LANES, LANES), F32),
        ],
        compiler_params=pltpu.CompilerParams(vmem_limit_bytes=LIMIT),
        cost_estimate=pl.CostEstimate(flops=2 * dots, bytes_accessed=8 << 20, transcendentals=0),
        name="own_rows",
    )(order, turns, coeffs, waves, levels, fast, fast_levels)
    total, parts = [], []
    for g in range(groups):
        last = g == groups - 1
        args = [slow[g], slow_levels, levels, lhs, tiles, edge, middle, *total]
        shapes = [(2, block, width), (2, 2, group, block, width)]
        scratch = [pltpu.VMEM((2 * block, width), F32), pltpu.VMEM((2, LANES, LANES), F32)]
        outs = shapes
        if last:
            args += [own_done, own_sum, *parts]
            outs = [waves.shape, (STEPS, rows, width)]
            scratch = [pltpu.VMEM(shape, F32) for shape in shapes] + scratch
            scratch.append(pltpu.SemaphoreType.DMA((groups + group + 5,)))
        result = pl.pallas_call(
            functools.partial(second_kernel, g * group, g == 0, last),
            out_shape=[jax.ShapeDtypeStruct(shape, F32) for shape in outs],
            in_specs=[VMEM] * len(args),
            out_specs=[ANY if last else VMEM] * len(outs),
            scratch_shapes=scratch,
            compiler_params=pltpu.CompilerParams(vmem_limit_bytes=LIMIT),
            cost_estimate=pl.CostEstimate(flops=dots // groups, bytes_accessed=4 << 20, transcendentals=0),
            name=f"edge_rows_{g}",
        )(*args)
        total = result[:1]
        parts.append(result[1])
    return tuple(result)


def solution(mesh):
    in_specs = (P(None, None, "shot", "strip", None), P("strip", None), P(), P(), P("shot"))
    out_specs = (P(None, None, "shot", "strip", None), P("shot", "strip", None))
    return jax.shard_map(
        on_device, mesh=mesh, in_specs=in_specs, out_specs=out_specs, check_vma=False
    )
```

```python
import functools

import jax
import jax.numpy as jnp
from jax import lax
from jax.experimental import pallas as pl
from jax.experimental.pallas import tpu as pltpu
from jax.sharding import PartitionSpec as P

STEPS = 2
LANES = 128
F32 = jnp.float32
BF16 = jnp.bfloat16


def pick(values, masks):
    out = values[0]
    for value, mask in zip(values[1:], masks):
        out = jnp.where(mask, value, out)
    return out


def level_masks(level, count):
    return [level == float(l) for l in range(1, count)]


def split(cells):
    high = cells.astype(BF16)
    return high, (cells - high.astype(F32)).astype(BF16)


def build_filters(coef_ref, row_of, pad_ref, lhs_ref, wanted, block):
    levels, taps = coef_ref.shape[2:]
    pad_ref[...] = jnp.zeros_like(pad_ref)
    pad_ref[:, :, :levels, :taps] = coef_ref[...]
    wide = 2 * block
    for n, f in enumerate(wanted):
        row = row_of(f)
        real, imag = pad_ref[0, row], pad_ref[1, row]
        tables = (real - pltpu.roll(imag, wide, 1), imag + pltpu.roll(real, wide, 1))
        tables = [table + pltpu.roll(table, 2 * wide, 1) for table in tables]
        for level in range(levels):
            for part in range(2):
                line = jnp.broadcast_to(tables[part][level : level + 1], (block, LANES))
                high, low = split(pltpu.roll(line, 0, 1, stride=1, stride_axis=0))
                at = (level * 2 + part) * block
                lhs_ref[n, at : at + block, :LANES] = high
                lhs_ref[n, at : at + block, LANES:] = low


def band_product(lhs, reals, imags):
    rhs = jnp.concatenate([reals[0], imags[0], reals[1], imags[1], reals[0], imags[0]], axis=0)
    return jnp.dot(lhs[:, : rhs.shape[0]], rhs, preferred_element_type=F32)


def band_pick(found, masks, block):
    count = found.shape[0] // (2 * block)
    return [
        pick([found[(l * 2 + part) * block : (l * 2 + part + 1) * block] for l in range(count)], masks)
        for part in range(2)
    ]


def turn_tables(turn_ref, f, masks):
    height, width = masks[0].shape
    tables = []
    for part in range(2):
        values = []
        for l in range(len(masks) + 1):
            tile = turn_ref[f, part, l]
            tile = jnp.concatenate([tile] * (height // tile.shape[0]), axis=0)
            values.append(jnp.concatenate([tile] * (width // LANES), axis=1))
        tables.append(pick(values, masks))
    return tables


def rotate(cells, cosine, sine):
    real, imag = cells
    return real * cosine - imag * sine, real * sine + imag * cosine


def to_columns(fields, block):
    chunks = fields[0].shape[1] // LANES
    return jnp.concatenate(
        [field[:, c * LANES : (c + 1) * LANES] for c in range(chunks) for field in fields], axis=0
    ).T


def inline(lhs, fields, masks_t, block):
    half = block // 2
    count = len(fields)
    chunks = fields[0][0].shape[1] // LANES
    step = count * block
    lane = lax.broadcasted_iota(jnp.int32, (half, LANES), 1)
    columns = []
    for part in range(2):
        columns.append(to_columns([field[part] for field in fields], block))
        yield
    parts = []
    for cols in columns:
        before = jnp.where(lane < step, 0.0, pltpu.roll(cols[LANES - half :], step, 1))
        after = jnp.where(lane >= LANES - step, 0.0, pltpu.roll(cols[:half], LANES - step, 1))
        parts.append(split(jnp.concatenate([before, cols, after], axis=0)))
        yield
    mid = LANES // 2
    halves = [[[], []], [[], []]]
    masks_t = masks_t()
    found = []
    spots = list(range(0, mid, block))

    def finish(at):
        masks = [jnp.concatenate([m[at : at + block], m[mid + at : mid + at + block]], axis=1) for m in masks_t]
        got = band_pick(found.pop(0), masks, block)
        for part in range(2):
            halves[part][0].append(got[part][:, :LANES])
            halves[part][1].append(got[part][:, LANES:])

    for n, at in enumerate(spots):
        windows = [
            [
                jnp.concatenate([x[at : at + 2 * block], x[mid + at : mid + at + 2 * block]], axis=1)
                for x in parts[part]
            ]
            for part in range(2)
        ]
        found.append(band_product(lhs, windows[0], windows[1]))
        yield
        if n >= LAG:
            finish(spots[n - LAG])
    for at in spots[len(spots) - LAG :]:
        finish(at)
    yield
    back = []
    for part in range(2):
        back.append(jnp.concatenate(halves[part][0] + halves[part][1], axis=0).T)
        yield
    return [
        [
            jnp.concatenate(
                [back[part][(c * count + i) * block : (c * count + i + 1) * block] for c in range(chunks)], axis=1
            )
            for part in range(2)
        ]
        for i in range(count)
    ]


def split_fields(fields):
    return [list(zip(*[split(cells) for cells in field])) for field in fields]


def saved(ref, f):
    return [[[ref[f, i, kind, part] for part in range(2)] for kind in range(2)] for i in range(2)]


def save(ref, f, blocks):
    for i in range(2):
        for kind in range(2):
            for part in range(2):
                ref[f, i, kind, part] = blocks[i][kind][part]


def ordered(swap, first, second):
    both = [
        [[(jnp.where(swap, y, x), jnp.where(swap, x, y)) for x, y in zip(p, q)] for p, q in zip(a, b)]
        for a, b in zip(first, second)
    ]
    return [[[[pair[n] for pair in kind] for kind in field] for field in both] for n in range(2)]


def crossline(lhs, first, second, masks, block):
    wide = 2 * LANES
    width = first[0][0][0].shape[1]
    pieces = [[[], []], [[], []]]
    spots = [(i, at) for i in range(2) for at in range(0, width, wide)]
    found = []

    def finish(spot):
        i, at = spot
        got = band_pick(found.pop(0), [m[:, at : at + wide] for m in masks], block)
        for part in range(2):
            pieces[i][part].append(got[part])

    for n, (i, at) in enumerate(spots):
        windows = [
            [
                jnp.concatenate([b[i][kind][part][:, at : at + wide] for b in (first, second)], axis=0)
                for kind in range(2)
            ]
            for part in range(2)
        ]
        found.append(band_product(lhs, windows[0], windows[1]))
        yield
        if n >= LAG:
            finish(spots[n - LAG])
    for spot in spots[len(spots) - LAG :]:
        finish(spot)
    yield
    return [[jnp.concatenate(p, axis=1) for p in piece] for piece in pieces]


def interleave(chains, skew):
    live = dict(enumerate(chains))
    tick = 0
    while live:
        for n in list(live):
            if tick >= n * skew and next(live[n], live) is live:
                del live[n]
        tick += 1


def image_of(fields):
    (sr, si), (qr, qi) = fields
    return sr * qr - si * qi


def raw_fields(get, cosine, sine):
    fields = [[get(i, p) for p in range(2)] for i in range(2)]
    fields[1][1] = -fields[1][1]
    return [rotate(field, cosine, sine) for field in fields]


def put_done(done_ref, f, fields):
    (sr, si), (qr, qi) = fields
    done_ref[0, 0, f], done_ref[0, 1, f], done_ref[1, 0, f], done_ref[1, 1, f] = sr, si, qr, -qi


def window_levels(ref, inner, outer, inner_at, block):
    ref[pl.ds(pl.multiple_of(inner_at, block), block)] = inner
    ref[pl.ds(pl.multiple_of(block - inner_at, block), block)] = outer
    return ref[block // 2 : block // 2 + block]


def first_kernel(
    meta_ref, coef_ref, waves_ref, lev_ref, fast_ref, halo_ref,
    done_ref, acc_ref, edge_ref, mid_ref, lhs_ref, turn_ref,
    pad_ref, levw_ref, levt_ref,
):
    freqs = lhs_ref.shape[0]
    levels, taps = coef_ref.shape[2:]
    block = taps - 1
    half = block // 2
    c = lax.axis_index("strip") % 2

    def row_of(f):
        return meta_ref[2 * freqs * levels + f].astype(jnp.int32)

    for f in range(freqs):
        for part in range(2):
            for l in range(levels):
                turn_ref[f, part, l] = jnp.full(turn_ref.shape[3:], meta_ref[(part * freqs + row_of(f)) * levels + l], F32)
    build_filters(coef_ref, row_of, pad_ref, lhs_ref, range(freqs), block)
    slow_row = pl.multiple_of(block * c, block)
    fast_row = pl.multiple_of(block * (1 - c), block)
    lev_slow = lev_ref[pl.ds(slow_row, block)].astype(F32)
    lev_fast = lev_ref[pl.ds(fast_row, block)].astype(F32)
    lev_halo = halo_ref[...].astype(F32)
    lev_mid = lev_ref[half : half + block].astype(F32)
    lev_edge = window_levels(levw_ref, lev_fast, lev_halo, block * c, block)
    blocks = (lev_slow, lev_fast, lev_halo, lev_mid, lev_edge)
    for slot, lev in enumerate(blocks):
        levt_ref[slot] = to_columns([lev, lev], block)
    masks = [level_masks(lev, levels) for lev in blocks]
    acc_ref[...] = jnp.zeros_like(acc_ref)
    ready = {}

    def start_chain(f, slot):
        cosine, sine = turn_tables(turn_ref, f, masks[slot])
        if slot < 2:
            at = (slow_row, fast_row)[slot]
            get = lambda i, p: waves_ref[i, p, f, pl.ds(at, block)]
        else:
            get = lambda i, p: fast_ref[(i * 2 + p) * freqs + f]
        fields = raw_fields(get, cosine, sine)
        yield
        fields = yield from inline(lhs_ref[f], fields, lambda: level_masks(levt_ref[slot], levels), block)
        ready[f, slot] = split_fields(fields)
        if slot == 0:
            save(edge_ref, f, ready[f, slot])

    def next_chain(f, slot):
        first, second = ((0, 1), (1, 2))[slot]
        fields = yield from crossline(lhs_ref[f], *ordered(c == 1, ready[f, first], ready[f, second]), masks[3 + slot], block)
        acc_ref[slot] += image_of(fields)
        cosine, sine = turn_tables(turn_ref, f, masks[3 + slot])
        fields = [rotate(field, cosine, sine) for field in fields]
        yield
        fields = yield from inline(lhs_ref[f], fields, lambda: level_masks(levt_ref[3 + slot], levels), block)
        ready[f, 3 + slot] = split_fields(fields)
        if slot == 0:
            save(mid_ref, f, ready[f, 3])

    def last_chain(f):
        fields = yield from crossline(lhs_ref[f], *ordered(c == 1, ready[f, 3], ready[f, 4]), masks[1], block)
        acc_ref[2] += image_of(fields)
        put_done(done_ref, f, fields)

    interleave([start_chain(f, slot) for f in range(freqs) for slot in range(3)], SKEW1)
    interleave([next_chain(f, slot) for f in range(freqs) for slot in range(2)], SKEW1)
    interleave([last_chain(f) for f in range(freqs)], SKEW1)


def second_kernel(
    offset, first, last,
    slow_ref, halo_ref, lev_ref, lhs_ref, turn_ref, edge_ref, mid_ref, *refs,
):
    refs = list(refs)
    sum_in_ref = None if first else refs.pop(0)
    if last:
        out_ref, img_ref, sum_ref, done_ref, levw_ref, levt_ref, sem = refs[-7:]
        own_ref, own_sum_ref, *before = refs[:-7]
    else:
        sum_ref, done_ref, levw_ref, levt_ref = refs
    levels = turn_ref.shape[2]
    block = lhs_ref.shape[1] // (2 * levels)
    group = done_ref.shape[2]
    half = block // 2
    rows = lev_ref.shape[0]
    index = lax.axis_index("strip")
    c = index % 2
    outside = jnp.where(c == 0, index == 0, index == lax.axis_size("strip") - 1)
    inside = jnp.where(outside, 0.0, 1.0).astype(F32)
    slow_row = pl.multiple_of(block * c, block)
    lev_near = lev_ref[pl.ds(slow_row, block)].astype(F32)
    lev_halo = halo_ref[...].astype(F32)
    lev_edge = window_levels(levw_ref, lev_near, lev_halo, block * (1 - c), block)
    for slot, lev in enumerate((lev_halo, lev_edge)):
        levt_ref[slot] = to_columns([lev, lev], block)
    masks_near, masks_halo, masks_edge = [level_masks(lev, levels) for lev in (lev_near, lev_halo, lev_edge)]
    line = lax.broadcasted_iota(jnp.int32, lev_edge.shape, 0)
    keep = jnp.where((line >= half) == (c == 0), 1.0, inside)
    sum_ref[...] = jnp.zeros_like(sum_ref) if first else sum_in_ref[...]
    copies = []

    def send(source, target):
        copies.append(pltpu.make_async_copy(source, target, sem.at[len(copies)]))
        copies[-1].start()

    if last:
        fast_row = pl.multiple_of(block * (1 - c), block)
        own_half = pl.ds(pl.multiple_of(half * c, half), half)
        own_edge = pl.ds(pl.multiple_of((rows - half) * (1 - c), half), half)
        send(own_ref, out_ref.at[:, :, :, pl.ds(fast_row, block)])
        for n, ref in enumerate(before):
            send(ref, out_ref.at[:, :, pl.ds(n * group, group), pl.ds(slow_row, block)])
        send(own_sum_ref.at[0], img_ref.at[0, pl.ds(half, block)])
        send(own_sum_ref.at[1, own_half], img_ref.at[0, own_edge])
        send(own_sum_ref.at[2], img_ref.at[1, pl.ds(fast_row, block)])

    def chain(g):
        f = offset + g
        cosine, sine = [inside * t for t in turn_tables(turn_ref, f, masks_halo)]
        get = lambda i, p: slow_ref[(i * 2 + p) * group + g]
        fields = raw_fields(get, cosine, sine)
        yield
        fields = yield from inline(lhs_ref[f], fields, lambda: level_masks(levt_ref[0], levels), block)
        outer = split_fields(fields)
        yield
        fields = yield from crossline(lhs_ref[f], *ordered(c == 0, saved(edge_ref, f), outer), masks_edge, block)
        sum_ref[0] += image_of(fields)
        cosine, sine = [keep * t for t in turn_tables(turn_ref, f, masks_edge)]
        fields = [rotate(field, cosine, sine) for field in fields]
        yield
        if last and g == group - 1:
            own_row = pl.multiple_of(half * (1 - c), half)
            edge_row = pl.multiple_of((rows - half) * c, half)
            send(sum_ref.at[0, pl.ds(own_row, half)], img_ref.at[0, pl.ds(edge_row, half)])
        fields = yield from inline(lhs_ref[f], fields, lambda: level_masks(levt_ref[1], levels), block)
        outer = split_fields(fields)
        yield
        fields = yield from crossline(lhs_ref[f], *ordered(c == 0, saved(mid_ref, f), outer), masks_near, block)
        sum_ref[1] += image_of(fields)
        put_done(done_ref, g, fields)
        if last:
            send(done_ref.at[:, :, g], out_ref.at[:, :, f, pl.ds(slow_row, block)])

    interleave([chain(g) for g in range(group)], SKEW)
    if last:
        send(sum_ref.at[1], img_ref.at[1, pl.ds(slow_row, block)])
    for copy in copies:
        copy.wait()


VMEM = pl.BlockSpec(memory_space=pltpu.VMEM)
SMEM = pl.BlockSpec(memory_space=pltpu.SMEM)
ANY = pl.BlockSpec(memory_space=pl.ANY)
LIMIT = 48 * 1024 * 1024
SKEW = 3
SKEW1 = 2
LAG = 1
GROUPS = 2


def on_device(waves, levels, coeffs, angles, order):
    freqs = order.shape[0]
    rows, width = levels.shape
    level_count, taps = coeffs.shape[2:]
    block = taps - 1
    count = lax.axis_size("strip")
    index = lax.axis_index("strip")
    c = index % 2
    groups = GROUPS if freqs % GROUPS == 0 else 1
    group = freqs // groups

    def side(cells, start, low=0, high=freqs):
        cells = lax.dynamic_slice_in_dim(cells, start, block, axis=3)
        return cells[:, :, low:high].reshape(-1, block, width)

    shots = lax.axis_size("shot")
    across, within = [], []
    for shot in range(shots):
        for i in range(count):
            j = i + 1 if i % 2 else i - 1
            other = shot if 0 <= j < count else min(shot ^ 1, shots - 1)
            across.append((shot * count + i, other * count + (j if 0 <= j < count else i)))
            within.append((shot * count + i, shot * count + (i ^ 1)))
    axes = ("shot", "strip")

    slow_row, fast_row = c * (rows - block), (1 - c) * (rows - block)
    slow = [lax.ppermute(side(waves, slow_row, 0, group), axes, across)]
    near = side(waves, fast_row)
    fast = lax.ppermute(near, axes, within)
    cells, marks, _ = lax.optimization_barrier((waves, levels, near))
    fast_levels = lax.ppermute(lax.dynamic_slice_in_dim(marks, fast_row, block, axis=0), axes, within)
    slow_levels = lax.ppermute(lax.dynamic_slice_in_dim(marks, slow_row, block, axis=0), axes, across)
    for g in range(1, groups):
        slow.append(lax.ppermute(side(cells, slow_row, g * group, (g + 1) * group), axes, across))

    meta = jnp.concatenate([jnp.cos(angles).ravel(), jnp.sin(angles).ravel(), order.astype(F32)])
    lhs_shape = (freqs, 2 * level_count * block, 2 * LANES)
    state = (freqs, 2, 2, 2, block, width)
    dots = 16 * freqs * 2 * lhs_shape[1] * 12 * block * width
    own_done, own_sum, edge, middle, lhs, tiles = pl.pallas_call(
        first_kernel,
        out_shape=[
            jax.ShapeDtypeStruct((2, 2, freqs, block, width), F32),
            jax.ShapeDtypeStruct((3, block, width), F32),
            jax.ShapeDtypeStruct(state, BF16),
            jax.ShapeDtypeStruct(state, BF16),
            jax.ShapeDtypeStruct(lhs_shape, BF16),
            jax.ShapeDtypeStruct((freqs, 2, level_count, 8, LANES), F32),
        ],
        in_specs=[SMEM, VMEM, VMEM, VMEM, VMEM, VMEM],
        out_specs=[VMEM] * 6,
        scratch_shapes=[
            pltpu.VMEM(coeffs.shape[:2] + (8, LANES), F32),
            pltpu.VMEM((2 * block, width), F32),
            pltpu.VMEM((5, LANES, LANES), F32),
        ],
        compiler_params=pltpu.CompilerParams(vmem_limit_bytes=LIMIT),
        cost_estimate=pl.CostEstimate(flops=2 * dots, bytes_accessed=8 << 20, transcendentals=0),
        name="own_rows",
    )(meta, coeffs, waves, levels, fast, fast_levels)
    total, parts = [], []
    for g in range(groups):
        last = g == groups - 1
        args = [slow[g], slow_levels, levels, lhs, tiles, edge, middle, *total]
        shapes = [(2, block, width), (2, 2, group, block, width)]
        scratch = [pltpu.VMEM((2 * block, width), F32), pltpu.VMEM((2, LANES, LANES), F32)]
        outs = shapes
        if last:
            args += [own_done, own_sum, *parts]
            outs = [waves.shape, (STEPS, rows, width)]
            scratch = [pltpu.VMEM(shape, F32) for shape in shapes] + scratch
            scratch.append(pltpu.SemaphoreType.DMA((groups + group + 5,)))
        result = pl.pallas_call(
            functools.partial(second_kernel, g * group, g == 0, last),
            out_shape=[jax.ShapeDtypeStruct(shape, F32) for shape in outs],
            in_specs=[VMEM] * len(args),
            out_specs=[ANY if last else VMEM] * len(outs),
            scratch_shapes=scratch,
            compiler_params=pltpu.CompilerParams(vmem_limit_bytes=LIMIT),
            cost_estimate=pl.CostEstimate(flops=dots // groups, bytes_accessed=4 << 20, transcendentals=0),
            name=f"edge_rows_{g}",
        )(*args)
        total = result[:1]
        parts.append(result[1])
    return tuple(result)


def solution(mesh):
    in_specs = (P(None, None, "shot", "strip", None), P("strip", None), P(), P(), P("shot"))
    out_specs = (P(None, None, "shot", "strip", None), P("shot", "strip", None))
    return jax.shard_map(
        on_device, mesh=mesh, in_specs=in_specs, out_specs=out_specs, check_vma=False
    )
```

```python
import functools

import jax
import jax.numpy as jnp
from jax import lax
from jax.experimental import pallas as pl
from jax.experimental.pallas import tpu as pltpu
from jax.sharding import PartitionSpec as P

STEPS = 2
LANES = 128
F32 = jnp.float32
BF16 = jnp.bfloat16


def pick(values, masks):
    out = values[0]
    for value, mask in zip(values[1:], masks):
        out = jnp.where(mask, value, out)
    return out


def level_masks(level, count):
    return [level == float(l) for l in range(1, count)]


def split(cells):
    high = cells.astype(BF16)
    return high, (cells - high.astype(F32)).astype(BF16)


def build_filters(coef_ref, row_of, pad_ref, lhs_ref, wanted, block):
    levels = lhs_ref.shape[1] // (2 * block)
    pad_ref = coef_ref
    wide = 2 * block
    for n, f in enumerate(wanted):
        row = row_of(f)
        real, imag = pad_ref[0, row], pad_ref[1, row]
        tables = (real - pltpu.roll(imag, wide, 1), imag + pltpu.roll(real, wide, 1))
        tables = [table + pltpu.roll(table, 2 * wide, 1) for table in tables]
        for level in range(levels):
            for part in range(2):
                line = jnp.broadcast_to(tables[part][level : level + 1], (block, LANES))
                high, low = split(pltpu.roll(line, 0, 1, stride=1, stride_axis=0))
                at = (level * 2 + part) * block
                lhs_ref[n, at : at + block, :LANES] = high
                lhs_ref[n, at : at + block, LANES:] = low


def band_product(lhs, reals, imags):
    rhs = jnp.concatenate([reals[0], imags[0], reals[1], imags[1], reals[0], imags[0]], axis=0)
    return jnp.dot(lhs[:, : rhs.shape[0]], rhs, preferred_element_type=F32)


def band_pick(found, masks, block):
    count = found.shape[0] // (2 * block)
    return [
        pick([found[(l * 2 + part) * block : (l * 2 + part + 1) * block] for l in range(count)], masks)
        for part in range(2)
    ]


def turn_tables(turn_ref, f, masks):
    height, width = masks[0].shape
    tables = []
    for part in range(2):
        values = []
        for l in range(len(masks) + 1):
            tile = turn_ref[f, part, l]
            tile = jnp.concatenate([tile] * (height // tile.shape[0]), axis=0)
            values.append(jnp.concatenate([tile] * (width // LANES), axis=1))
        tables.append(pick(values, masks))
    return tables


def rotate(cells, cosine, sine):
    real, imag = cells
    return real * cosine - imag * sine, real * sine + imag * cosine


def to_columns(fields, block):
    chunks = fields[0].shape[1] // LANES
    return jnp.concatenate(
        [field[:, c * LANES : (c + 1) * LANES] for c in range(chunks) for field in fields], axis=0
    ).T


def inline(lhs, fields, masks_t, block):
    half = block // 2
    count = len(fields)
    chunks = fields[0][0].shape[1] // LANES
    step = count * block
    lane = lax.broadcasted_iota(jnp.int32, (half, LANES), 1)
    columns = []
    for part in range(2):
        columns.append(to_columns([field[part] for field in fields], block))
        yield
    parts = []
    for cols in columns:
        before = jnp.where(lane < step, 0.0, pltpu.roll(cols[LANES - half :], step, 1))
        after = jnp.where(lane >= LANES - step, 0.0, pltpu.roll(cols[:half], LANES - step, 1))
        parts.append(split(jnp.concatenate([before, cols, after], axis=0)))
        yield
    mid = LANES // 2
    halves = [[[], []], [[], []]]
    masks_t = masks_t()
    found = []
    spots = list(range(0, mid, block))

    def finish(at):
        masks = [jnp.concatenate([m[at : at + block], m[mid + at : mid + at + block]], axis=1) for m in masks_t]
        got = band_pick(found.pop(0), masks, block)
        for part in range(2):
            halves[part][0].append(got[part][:, :LANES])
            halves[part][1].append(got[part][:, LANES:])

    for n, at in enumerate(spots):
        windows = [
            [
                jnp.concatenate([x[at : at + 2 * block], x[mid + at : mid + at + 2 * block]], axis=1)
                for x in parts[part]
            ]
            for part in range(2)
        ]
        found.append(band_product(lhs, windows[0], windows[1]))
        yield
        if n >= LAG:
            finish(spots[n - LAG])
    for at in spots[len(spots) - LAG :]:
        finish(at)
    yield
    back = []
    for part in range(2):
        back.append(jnp.concatenate(halves[part][0] + halves[part][1], axis=0).T)
        yield
    return [
        [
            jnp.concatenate(
                [back[part][(c * count + i) * block : (c * count + i + 1) * block] for c in range(chunks)], axis=1
            )
            for part in range(2)
        ]
        for i in range(count)
    ]


def split_fields(fields):
    return [list(zip(*[split(cells) for cells in field])) for field in fields]


def saved(ref, f):
    return [[[ref[f, i, kind, part] for part in range(2)] for kind in range(2)] for i in range(2)]


def save(ref, f, blocks):
    for i in range(2):
        for kind in range(2):
            for part in range(2):
                ref[f, i, kind, part] = blocks[i][kind][part]


def ordered(swap, first, second):
    both = [
        [[(jnp.where(swap, y, x), jnp.where(swap, x, y)) for x, y in zip(p, q)] for p, q in zip(a, b)]
        for a, b in zip(first, second)
    ]
    return [[[[pair[n] for pair in kind] for kind in field] for field in both] for n in range(2)]


def crossline(lhs, first, second, masks, block):
    wide = 2 * LANES
    width = first[0][0][0].shape[1]
    pieces = [[[], []], [[], []]]
    spots = [(i, at) for i in range(2) for at in range(0, width, wide)]
    found = []

    def finish(spot):
        i, at = spot
        got = band_pick(found.pop(0), [m[:, at : at + wide] for m in masks], block)
        for part in range(2):
            pieces[i][part].append(got[part])

    for n, (i, at) in enumerate(spots):
        windows = [
            [
                jnp.concatenate([b[i][kind][part][:, at : at + wide] for b in (first, second)], axis=0)
                for kind in range(2)
            ]
            for part in range(2)
        ]
        found.append(band_product(lhs, windows[0], windows[1]))
        yield
        if n >= LAG:
            finish(spots[n - LAG])
    for spot in spots[len(spots) - LAG :]:
        finish(spot)
    yield
    return [[jnp.concatenate(p, axis=1) for p in piece] for piece in pieces]


def interleave(chains, skew):
    live = dict(enumerate(chains))
    tick = 0
    while live:
        for n in list(live):
            if tick >= n * skew and next(live[n], live) is live:
                del live[n]
        tick += 1


def image_of(fields):
    (sr, si), (qr, qi) = fields
    return sr * qr - si * qi


def raw_fields(get, cosine, sine):
    fields = [[get(i, p) for p in range(2)] for i in range(2)]
    fields[1][1] = -fields[1][1]
    return [rotate(field, cosine, sine) for field in fields]


def put_done(done_ref, f, fields):
    (sr, si), (qr, qi) = fields
    done_ref[0, 0, f], done_ref[0, 1, f], done_ref[1, 0, f], done_ref[1, 1, f] = sr, si, qr, -qi


def window_levels(ref, inner, outer, inner_at, block):
    ref[pl.ds(pl.multiple_of(inner_at, block), block)] = inner
    ref[pl.ds(pl.multiple_of(block - inner_at, block), block)] = outer
    return ref[block // 2 : block // 2 + block]


def early_kernel(
    meta_ref, coef_ref, raw_ref, lev_ref,
    sent_ref, edge_ref, lhs_ref, turn_ref,
    pad_ref, levt_ref,
):
    freqs = turn_ref.shape[0]
    block = raw_ref.shape[1]
    levels = lhs_ref.shape[1] // (2 * block)
    later = edge_ref.shape[0]
    c = lax.axis_index("strip") % 2

    def row_of(f):
        return meta_ref[2 * freqs * levels + f].astype(jnp.int32)

    for f in range(freqs):
        for part in range(2):
            for l in range(levels):
                turn_ref[f, part, l] = jnp.full(
                    turn_ref.shape[3:], meta_ref[(part * freqs + row_of(f)) * levels + l], F32
                )
    build_filters(coef_ref, row_of, pad_ref, lhs_ref, range(freqs - later, freqs), block)
    slow_row = pl.multiple_of(block * c, block)
    lev = lev_ref[pl.ds(slow_row, block)].astype(F32)
    levt_ref[...] = to_columns([lev, lev], block)
    masks = level_masks(lev, levels)

    def chain(n):
        f = freqs - later + n
        cosine, sine = turn_tables(turn_ref, f, masks)
        fields = raw_fields(lambda i, p: raw_ref[(i * 2 + p) * later + n], cosine, sine)
        yield
        fields = yield from inline(lhs_ref[n], fields, lambda: level_masks(levt_ref[...], levels), block)
        for i in range(2):
            for p in range(2):
                sent_ref[(i * 2 + p) * later + n] = fields[i][p]
        save(edge_ref, n, split_fields(fields))

    interleave([chain(n) for n in range(later)], SKEW1)


def first_kernel(
    meta_ref, coef_ref, waves_ref, lev_ref, fast_ref, halo_ref, early_lhs_ref, turn_ref, later_ref,
    done_ref, acc_ref, edge_ref, mid_ref, lhs_ref,
    pad_ref, levw_ref, levt_ref,
):
    freqs = lhs_ref.shape[0]
    levels = turn_ref.shape[2]
    block = lhs_ref.shape[1] // (2 * levels)
    group = edge_ref.shape[0]
    half = block // 2
    c = lax.axis_index("strip") % 2

    def row_of(f):
        return meta_ref[2 * freqs * levels + f].astype(jnp.int32)

    build_filters(coef_ref, row_of, pad_ref, lhs_ref, range(group), block)
    for f in range(group, freqs):
        lhs_ref[f] = early_lhs_ref[f - group]
    slow_row = pl.multiple_of(block * c, block)
    fast_row = pl.multiple_of(block * (1 - c), block)
    lev_slow = lev_ref[pl.ds(slow_row, block)].astype(F32)
    lev_fast = lev_ref[pl.ds(fast_row, block)].astype(F32)
    lev_halo = halo_ref[...].astype(F32)
    lev_mid = lev_ref[half : half + block].astype(F32)
    lev_edge = window_levels(levw_ref, lev_fast, lev_halo, block * c, block)
    blocks = (lev_slow, lev_fast, lev_halo, lev_mid, lev_edge)
    for slot, lev in enumerate(blocks):
        levt_ref[slot] = to_columns([lev, lev], block)
    masks = [level_masks(lev, levels) for lev in blocks]
    acc_ref[...] = jnp.zeros_like(acc_ref)
    ready = {}

    def start_chain(f, slot):
        cosine, sine = turn_tables(turn_ref, f, masks[slot])
        if slot < 2:
            at = (slow_row, fast_row)[slot]
            get = lambda i, p: waves_ref[i, p, f, pl.ds(at, block)]
        else:
            get = lambda i, p: fast_ref[(i * 2 + p) * freqs + f]
        fields = raw_fields(get, cosine, sine)
        yield
        fields = yield from inline(lhs_ref[f], fields, lambda: level_masks(levt_ref[slot], levels), block)
        ready[f, slot] = split_fields(fields)
        if slot == 0:
            save(edge_ref, f, ready[f, slot])

    for f in range(group, freqs):
        ready[f, 0] = saved(later_ref, f - group)

    def next_chain(f, slot):
        first, second = ((0, 1), (1, 2))[slot]
        fields = yield from crossline(lhs_ref[f], *ordered(c == 1, ready[f, first], ready[f, second]), masks[3 + slot], block)
        acc_ref[slot] += image_of(fields)
        cosine, sine = turn_tables(turn_ref, f, masks[3 + slot])
        fields = [rotate(field, cosine, sine) for field in fields]
        yield
        fields = yield from inline(lhs_ref[f], fields, lambda: level_masks(levt_ref[3 + slot], levels), block)
        ready[f, 3 + slot] = split_fields(fields)
        if slot == 0:
            save(mid_ref, f, ready[f, 3])

    def last_chain(f):
        fields = yield from crossline(lhs_ref[f], *ordered(c == 1, ready[f, 3], ready[f, 4]), masks[1], block)
        acc_ref[2] += image_of(fields)
        put_done(done_ref, f, fields)

    interleave([start_chain(f, slot) for f in range(freqs) for slot in range(f >= group, 3)], SKEW1)
    interleave([next_chain(f, slot) for f in range(freqs) for slot in range(2)], SKEW1)
    interleave([last_chain(f) for f in range(freqs)], SKEW1)


def second_kernel(
    offset, first, last,
    slow_ref, halo_ref, lev_ref, lhs_ref, turn_ref, edge_ref, mid_ref, *refs,
):
    refs = list(refs)
    sum_in_ref = None if first else refs.pop(0)
    if last:
        out_ref, img_ref, sum_ref, done_ref, levw_ref, levt_ref, sem = refs[-7:]
        own_ref, own_sum_ref, *before = refs[:-7]
    else:
        sum_ref, done_ref, levw_ref, levt_ref = refs
    levels = turn_ref.shape[2]
    block = lhs_ref.shape[1] // (2 * levels)
    group = done_ref.shape[2]
    half = block // 2
    rows = lev_ref.shape[0]
    index = lax.axis_index("strip")
    c = index % 2
    outside = jnp.where(c == 0, index == 0, index == lax.axis_size("strip") - 1)
    inside = jnp.where(outside, 0.0, 1.0).astype(F32)
    slow_row = pl.multiple_of(block * c, block)
    lev_near = lev_ref[pl.ds(slow_row, block)].astype(F32)
    lev_halo = halo_ref[...].astype(F32)
    lev_edge = window_levels(levw_ref, lev_near, lev_halo, block * (1 - c), block)
    for slot, lev in enumerate((lev_halo, lev_edge)):
        levt_ref[slot] = to_columns([lev, lev], block)
    masks_near, masks_halo, masks_edge = [level_masks(lev, levels) for lev in (lev_near, lev_halo, lev_edge)]
    line = lax.broadcasted_iota(jnp.int32, lev_edge.shape, 0)
    keep = jnp.where((line >= half) == (c == 0), 1.0, inside)
    sum_ref[...] = jnp.zeros_like(sum_ref) if first else sum_in_ref[...]
    copies = []

    def send(source, target):
        copies.append(pltpu.make_async_copy(source, target, sem.at[len(copies)]))
        copies[-1].start()

    if last:
        fast_row = pl.multiple_of(block * (1 - c), block)
        own_half = pl.ds(pl.multiple_of(half * c, half), half)
        own_edge = pl.ds(pl.multiple_of((rows - half) * (1 - c), half), half)
        send(own_ref, out_ref.at[:, :, :, pl.ds(fast_row, block)])
        for n, ref in enumerate(before):
            send(ref, out_ref.at[:, :, pl.ds(n * group, group), pl.ds(slow_row, block)])
        send(own_sum_ref.at[0], img_ref.at[0, pl.ds(half, block)])
        send(own_sum_ref.at[1, own_half], img_ref.at[0, own_edge])
        send(own_sum_ref.at[2], img_ref.at[1, pl.ds(fast_row, block)])

    def chain(g):
        f = offset + g
        get = lambda i, p: slow_ref[(i * 2 + p) * group + g]
        if first:
            cosine, sine = [inside * t for t in turn_tables(turn_ref, f, masks_halo)]
            fields = raw_fields(get, cosine, sine)
            yield
            masks = lambda: level_masks(levt_ref[0], levels)
            fields = yield from inline(lhs_ref[f], fields, masks, block)
        else:
            fields = [[inside * get(i, p) for p in range(2)] for i in range(2)]
        outer = split_fields(fields)
        yield
        fields = yield from crossline(lhs_ref[f], *ordered(c == 0, saved(edge_ref, g), outer), masks_edge, block)
        sum_ref[0] += image_of(fields)
        cosine, sine = [keep * t for t in turn_tables(turn_ref, f, masks_edge)]
        fields = [rotate(field, cosine, sine) for field in fields]
        yield
        if last and g == group - 1:
            own_row = pl.multiple_of(half * (1 - c), half)
            edge_row = pl.multiple_of((rows - half) * c, half)
            send(sum_ref.at[0, pl.ds(own_row, half)], img_ref.at[0, pl.ds(edge_row, half)])
        fields = yield from inline(lhs_ref[f], fields, lambda: level_masks(levt_ref[1], levels), block)
        outer = split_fields(fields)
        yield
        fields = yield from crossline(lhs_ref[f], *ordered(c == 0, saved(mid_ref, f), outer), masks_near, block)
        sum_ref[1] += image_of(fields)
        put_done(done_ref, g, fields)
        if last:
            send(done_ref.at[:, :, g], out_ref.at[:, :, f, pl.ds(slow_row, block)])

    interleave([chain(g) for g in range(group)], SKEW)
    if last:
        send(sum_ref.at[1], img_ref.at[1, pl.ds(slow_row, block)])
    for copy in copies:
        copy.wait()


VMEM = pl.BlockSpec(memory_space=pltpu.VMEM)
SMEM = pl.BlockSpec(memory_space=pltpu.SMEM)
ANY = pl.BlockSpec(memory_space=pl.ANY)
LIMIT = 48 * 1024 * 1024
SKEW = 3
SKEW1 = 2
LAG = 1


def on_device(waves, levels, coeffs, angles, order):
    freqs = order.shape[0]
    rows, width = levels.shape
    level_count, taps = coeffs.shape[2:]
    block = taps - 1
    count = lax.axis_size("strip")
    index = lax.axis_index("strip")
    c = index % 2
    groups = 2
    group = freqs // groups

    def side(cells, start, low=0, high=freqs):
        cells = lax.dynamic_slice_in_dim(cells, start, block, axis=3)
        return cells[:, :, low:high].reshape(-1, block, width)

    shots = lax.axis_size("shot")
    across, within = [], []
    for shot in range(shots):
        for i in range(count):
            j = i + 1 if i % 2 else i - 1
            other = shot if 0 <= j < count else min(shot ^ 1, shots - 1)
            across.append((shot * count + i, other * count + (j if 0 <= j < count else i)))
            within.append((shot * count + i, shot * count + (i ^ 1)))
    axes = ("shot", "strip")

    slow_row, fast_row = c * (rows - block), (1 - c) * (rows - block)
    meta = jnp.concatenate([jnp.cos(angles).ravel(), jnp.sin(angles).ravel(), order.astype(F32)])
    lhs_shape = (freqs, 2 * level_count * block, 2 * LANES)
    state = (2, 2, 2, block, width)
    later = freqs - group
    dots = 16 * freqs * 2 * lhs_shape[1] * 12 * block * width
    taps_in = jnp.pad(coeffs, ((0, 0), (0, 0), (0, 8 - level_count), (0, LANES - taps)))
    far = side(waves, slow_row, 0, group)
    slow = [lax.ppermute(far, axes, across)]
    near = side(waves, fast_row)
    fast = lax.ppermute(near, axes, within)
    cells, marks, _ = lax.optimization_barrier((waves, levels, near))
    sent, later_edge, early_lhs, tiles = pl.pallas_call(
        early_kernel,
        out_shape=[
            jax.ShapeDtypeStruct((4 * later, block, width), F32),
            jax.ShapeDtypeStruct((later,) + state, BF16),
            jax.ShapeDtypeStruct((later,) + lhs_shape[1:], BF16),
            jax.ShapeDtypeStruct((freqs, 2, level_count, 8, LANES), F32),
        ],
        in_specs=[SMEM, VMEM, VMEM, VMEM],
        out_specs=[VMEM] * 4,
        scratch_shapes=[pltpu.VMEM(coeffs.shape[:2] + (8, LANES), F32), pltpu.VMEM((LANES, LANES), F32)],
        compiler_params=pltpu.CompilerParams(vmem_limit_bytes=LIMIT),
        cost_estimate=pl.CostEstimate(flops=dots // 8, bytes_accessed=2 << 20, transcendentals=0),
        name="early_rows",
    )(meta, taps_in, side(cells, slow_row, group, freqs), marks)
    fast_levels = lax.ppermute(lax.dynamic_slice_in_dim(marks, fast_row, block, axis=0), axes, within)
    slow_levels = lax.ppermute(lax.dynamic_slice_in_dim(marks, slow_row, block, axis=0), axes, across)
    slow.append(lax.ppermute(sent, axes, across))
    own_done, own_sum, edge, middle, lhs = pl.pallas_call(
        first_kernel,
        out_shape=[
            jax.ShapeDtypeStruct((2, 2, freqs, block, width), F32),
            jax.ShapeDtypeStruct((3, block, width), F32),
            jax.ShapeDtypeStruct((group,) + state, BF16),
            jax.ShapeDtypeStruct((freqs,) + state, BF16),
            jax.ShapeDtypeStruct(lhs_shape, BF16),
        ],
        in_specs=[SMEM] + [VMEM] * 8,
        out_specs=[VMEM] * 5,
        scratch_shapes=[pltpu.VMEM(coeffs.shape[:2] + (8, LANES), F32), pltpu.VMEM((2 * block, width), F32), pltpu.VMEM((5, LANES, LANES), F32)],
        compiler_params=pltpu.CompilerParams(vmem_limit_bytes=LIMIT),
        cost_estimate=pl.CostEstimate(flops=2 * dots, bytes_accessed=8 << 20, transcendentals=0),
        name="own_rows",
    )(meta, taps_in, cells, marks, fast, fast_levels, early_lhs, tiles, later_edge)
    edges = [edge, later_edge]
    total, parts = [], []
    for g in range(groups):
        last = g == groups - 1
        args = [slow[g], slow_levels, levels, lhs, tiles, edges[g], middle, *total]
        shapes = [(2, block, width), (2, 2, group, block, width)]
        scratch = [pltpu.VMEM((2 * block, width), F32), pltpu.VMEM((2, LANES, LANES), F32)]
        outs = shapes
        if last:
            args += [own_done, own_sum, *parts]
            outs = [waves.shape, (STEPS, rows, width)]
            scratch = [pltpu.VMEM(shape, F32) for shape in shapes] + scratch
            scratch.append(pltpu.SemaphoreType.DMA((groups + group + 5,)))
        result = pl.pallas_call(
            functools.partial(second_kernel, g * group, g == 0, last),
            out_shape=[jax.ShapeDtypeStruct(shape, F32) for shape in outs],
            in_specs=[VMEM] * len(args),
            out_specs=[ANY if last else VMEM] * len(outs),
            scratch_shapes=scratch,
            compiler_params=pltpu.CompilerParams(vmem_limit_bytes=LIMIT),
            cost_estimate=pl.CostEstimate(flops=dots // groups, bytes_accessed=4 << 20, transcendentals=0),
            name=f"edge_rows_{g}",
        )(*args)
        total = result[:1]
        parts.append(result[1])
    return tuple(result)


def solution(mesh):
    in_specs = (P(None, None, "shot", "strip", None), P("strip", None), P(), P(), P("shot"))
    out_specs = (P(None, None, "shot", "strip", None), P("shot", "strip", None))
    return jax.shard_map(
        on_device, mesh=mesh, in_specs=in_specs, out_specs=out_specs, check_vma=False
    )
```

```python
import functools

import jax
import jax.numpy as jnp
from jax import lax
from jax.experimental import pallas as pl
from jax.experimental.pallas import tpu as pltpu
from jax.sharding import PartitionSpec as P

STEPS = 2
LANES = 128
F32 = jnp.float32
BF16 = jnp.bfloat16


def pick(values, masks):
    out = values[0]
    for value, mask in zip(values[1:], masks):
        out = jnp.where(mask, value, out)
    return out


def level_masks(level, count):
    return [level == float(l) for l in range(1, count)]


def split(cells):
    high = cells.astype(BF16)
    return high, (cells - high.astype(F32)).astype(BF16)


def build_filters(coef_ref, row_of, pad_ref, lhs_ref, wanted, block):
    levels, taps = coef_ref.shape[2:]
    pad_ref[...] = jnp.zeros_like(pad_ref)
    pad_ref[:, :, :levels, :taps] = coef_ref[...]
    wide = 2 * block
    for n, f in enumerate(wanted):
        row = row_of(f)
        real, imag = pad_ref[0, row], pad_ref[1, row]
        tables = (real - pltpu.roll(imag, wide, 1), imag + pltpu.roll(real, wide, 1))
        tables = [table + pltpu.roll(table, 2 * wide, 1) for table in tables]
        for level in range(levels):
            for part in range(2):
                line = jnp.broadcast_to(tables[part][level : level + 1], (block, LANES))
                high, low = split(pltpu.roll(line, 0, 1, stride=1, stride_axis=0))
                at = (level * 2 + part) * block
                lhs_ref[n, at : at + block, :LANES] = high
                lhs_ref[n, at : at + block, LANES:] = low


def band_product(lhs, reals, imags):
    rhs = jnp.concatenate([reals[0], imags[0], reals[1], imags[1], reals[0], imags[0]], axis=0)
    return jnp.dot(lhs[:, : rhs.shape[0]], rhs, preferred_element_type=F32)


def band_pick(found, masks, block):
    count = found.shape[0] // (2 * block)
    return [
        pick([found[(l * 2 + part) * block : (l * 2 + part + 1) * block] for l in range(count)], masks)
        for part in range(2)
    ]


def turn_tables(turn_ref, f, masks):
    height, width = masks[0].shape
    tables = []
    for part in range(2):
        values = []
        for l in range(len(masks) + 1):
            tile = turn_ref[f, part, l]
            tile = jnp.concatenate([tile] * (height // tile.shape[0]), axis=0)
            values.append(jnp.concatenate([tile] * (width // LANES), axis=1))
        tables.append(pick(values, masks))
    return tables


def rotate(cells, cosine, sine):
    real, imag = cells
    return real * cosine - imag * sine, real * sine + imag * cosine


def to_columns(fields, block):
    chunks = fields[0].shape[1] // LANES
    return jnp.concatenate(
        [field[:, c * LANES : (c + 1) * LANES] for c in range(chunks) for field in fields], axis=0
    ).T


def inline(lhs, fields, masks_t, block):
    half = block // 2
    count = len(fields)
    chunks = fields[0][0].shape[1] // LANES
    step = count * block
    lane = lax.broadcasted_iota(jnp.int32, (half, LANES), 1)
    columns = []
    for part in range(2):
        columns.append(to_columns([field[part] for field in fields], block))
        yield
    parts = []
    for cols in columns:
        before = jnp.where(lane < step, 0.0, pltpu.roll(cols[LANES - half :], step, 1))
        after = jnp.where(lane >= LANES - step, 0.0, pltpu.roll(cols[:half], LANES - step, 1))
        parts.append(split(jnp.concatenate([before, cols, after], axis=0)))
        yield
    mid = LANES // 2
    halves = [[[], []], [[], []]]
    masks_t = masks_t()
    found = []
    spots = list(range(0, mid, block))

    def finish(at):
        masks = [jnp.concatenate([m[at : at + block], m[mid + at : mid + at + block]], axis=1) for m in masks_t]
        got = band_pick(found.pop(0), masks, block)
        for part in range(2):
            halves[part][0].append(got[part][:, :LANES])
            halves[part][1].append(got[part][:, LANES:])

    for n, at in enumerate(spots):
        windows = [
            [
                jnp.concatenate([x[at : at + 2 * block], x[mid + at : mid + at + 2 * block]], axis=1)
                for x in parts[part]
            ]
            for part in range(2)
        ]
        found.append(band_product(lhs, windows[0], windows[1]))
        yield
        if n >= LAG:
            finish(spots[n - LAG])
    for at in spots[len(spots) - LAG :]:
        finish(at)
    yield
    back = []
    for part in range(2):
        back.append(jnp.concatenate(halves[part][0] + halves[part][1], axis=0).T)
        yield
    return [
        [
            jnp.concatenate(
                [back[part][(c * count + i) * block : (c * count + i + 1) * block] for c in range(chunks)], axis=1
            )
            for part in range(2)
        ]
        for i in range(count)
    ]


def split_fields(fields):
    return [list(zip(*[split(cells) for cells in field])) for field in fields]


def saved(ref, f):
    return [[[ref[f, i, kind, part] for part in range(2)] for kind in range(2)] for i in range(2)]


def save(ref, f, blocks):
    for i in range(2):
        for kind in range(2):
            for part in range(2):
                ref[f, i, kind, part] = blocks[i][kind][part]


def ordered(swap, first, second):
    both = [
        [[(jnp.where(swap, y, x), jnp.where(swap, x, y)) for x, y in zip(p, q)] for p, q in zip(a, b)]
        for a, b in zip(first, second)
    ]
    return [[[[pair[n] for pair in kind] for kind in field] for field in both] for n in range(2)]


def crossline(lhs, first, second, masks, block, ready=None):
    wide = 2 * LANES
    width = first[0][0][0].shape[1]
    pieces = [[[], []], [[], []]]
    spots = [(i, at) for i in range(2) for at in range(0, width, wide)]
    found = []

    def finish(spot):
        i, at = spot
        got = band_pick(found.pop(0), [m[:, at : at + wide] for m in masks], block)
        for part in range(2):
            pieces[i][part].append(got[part])
        if ready is not None and at + wide == width:
            ready(i, *[jnp.concatenate(p, axis=1) for p in pieces[i]])

    for n, (i, at) in enumerate(spots):
        windows = [
            [
                jnp.concatenate([b[i][kind][part][:, at : at + wide] for b in (first, second)], axis=0)
                for kind in range(2)
            ]
            for part in range(2)
        ]
        found.append(band_product(lhs, windows[0], windows[1]))
        yield
        if n >= LAG:
            finish(spots[n - LAG])
    for spot in spots[len(spots) - LAG :]:
        finish(spot)
    yield
    return [[jnp.concatenate(p, axis=1) for p in piece] for piece in pieces]


def interleave(chains, skew):
    live = dict(enumerate(chains))
    tick = 0
    while live:
        for n in list(live):
            if tick >= n * skew and next(live[n], live) is live:
                del live[n]
        tick += 1


def image_of(fields):
    (sr, si), (qr, qi) = fields
    return sr * qr - si * qi


def raw_fields(get, cosine, sine):
    fields = [[get(i, p) for p in range(2)] for i in range(2)]
    fields[1][1] = -fields[1][1]
    return [rotate(field, cosine, sine) for field in fields]


def put_done(done_ref, f, i, real, imag):
    done_ref[i, 0, f] = real
    done_ref[i, 1, f] = -imag if i else imag


def window_levels(ref, inner, outer, inner_at, block):
    ref[pl.ds(pl.multiple_of(inner_at, block), block)] = inner
    ref[pl.ds(pl.multiple_of(block - inner_at, block), block)] = outer
    return ref[block // 2 : block // 2 + block]


def first_kernel(
    meta_ref, coef_ref, waves_ref, lev_ref, fast_ref, halo_ref,
    done_ref, acc_ref, edge_ref, mid_ref, lhs_ref, turn_ref,
    pad_ref, levw_ref, levt_ref,
):
    freqs = lhs_ref.shape[0]
    levels, taps = coef_ref.shape[2:]
    block = taps - 1
    half = block // 2
    c = lax.axis_index("strip") % 2

    def row_of(f):
        return meta_ref[2 * freqs * levels + f].astype(jnp.int32)

    for f in range(freqs):
        for part in range(2):
            for l in range(levels):
                turn_ref[f, part, l] = jnp.full(turn_ref.shape[3:], meta_ref[(part * freqs + row_of(f)) * levels + l], F32)
    build_filters(coef_ref, row_of, pad_ref, lhs_ref, range(freqs), block)
    slow_row = pl.multiple_of(block * c, block)
    fast_row = pl.multiple_of(block * (1 - c), block)
    lev_slow = lev_ref[pl.ds(slow_row, block)].astype(F32)
    lev_fast = lev_ref[pl.ds(fast_row, block)].astype(F32)
    lev_halo = halo_ref[...].astype(F32)
    lev_mid = lev_ref[half : half + block].astype(F32)
    lev_edge = window_levels(levw_ref, lev_fast, lev_halo, block * c, block)
    blocks = (lev_slow, lev_fast, lev_halo, lev_mid, lev_edge)
    for slot, lev in enumerate(blocks):
        levt_ref[slot] = to_columns([lev, lev], block)
    masks = [level_masks(lev, levels) for lev in blocks]
    acc_ref[...] = jnp.zeros_like(acc_ref)
    ready = {}

    def start_chain(f, slot):
        cosine, sine = turn_tables(turn_ref, f, masks[slot])
        if slot < 2:
            at = (slow_row, fast_row)[slot]
            get = lambda i, p: waves_ref[i, p, f, pl.ds(at, block)]
        else:
            get = lambda i, p: fast_ref[(i * 2 + p) * freqs + f]
        fields = raw_fields(get, cosine, sine)
        yield
        fields = yield from inline(lhs_ref[f], fields, lambda: level_masks(levt_ref[slot], levels), block)
        ready[f, slot] = split_fields(fields)
        if slot == 0:
            save(edge_ref, f, ready[f, slot])

    def next_chain(f, slot):
        first, second = ((0, 1), (1, 2))[slot]
        fields = yield from crossline(lhs_ref[f], *ordered(c == 1, ready[f, first], ready[f, second]), masks[3 + slot], block)
        acc_ref[slot] += image_of(fields)
        cosine, sine = turn_tables(turn_ref, f, masks[3 + slot])
        fields = [rotate(field, cosine, sine) for field in fields]
        yield
        fields = yield from inline(lhs_ref[f], fields, lambda: level_masks(levt_ref[3 + slot], levels), block)
        ready[f, 3 + slot] = split_fields(fields)
        if slot == 0:
            save(mid_ref, f, ready[f, 3])

    def last_chain(f):
        done = functools.partial(put_done, done_ref, f)
        fields = yield from crossline(lhs_ref[f], *ordered(c == 1, ready[f, 3], ready[f, 4]), masks[1], block, done)
        acc_ref[2] += image_of(fields)

    interleave([start_chain(f, slot) for f in range(freqs) for slot in range(3)], SKEW1)
    interleave([next_chain(f, slot) for f in range(freqs) for slot in range(2)], SKEW1)
    interleave([last_chain(f) for f in range(freqs)], SKEW1)


def second_kernel(
    offset, first, last,
    slow_ref, halo_ref, lev_ref, lhs_ref, turn_ref, edge_ref, mid_ref, *refs,
):
    refs = list(refs)
    sum_in_ref = None if first else refs.pop(0)
    if last:
        out_ref, img_ref, sum_ref, done_ref, levw_ref, levt_ref, sem = refs[-7:]
        own_ref, own_sum_ref, *before = refs[:-7]
    else:
        sum_ref, done_ref, levw_ref, levt_ref = refs
    levels = turn_ref.shape[2]
    block = lhs_ref.shape[1] // (2 * levels)
    group = done_ref.shape[2]
    half = block // 2
    rows = lev_ref.shape[0]
    index = lax.axis_index("strip")
    c = index % 2
    outside = jnp.where(c == 0, index == 0, index == lax.axis_size("strip") - 1)
    inside = jnp.where(outside, 0.0, 1.0).astype(F32)
    slow_row = pl.multiple_of(block * c, block)
    lev_near = lev_ref[pl.ds(slow_row, block)].astype(F32)
    lev_halo = halo_ref[...].astype(F32)
    lev_edge = window_levels(levw_ref, lev_near, lev_halo, block * (1 - c), block)
    for slot, lev in enumerate((lev_halo, lev_edge)):
        levt_ref[slot] = to_columns([lev, lev], block)
    masks_near, masks_halo, masks_edge = [level_masks(lev, levels) for lev in (lev_near, lev_halo, lev_edge)]
    line = lax.broadcasted_iota(jnp.int32, lev_edge.shape, 0)
    keep = jnp.where((line >= half) == (c == 0), 1.0, inside)
    sum_ref[...] = jnp.zeros_like(sum_ref) if first else sum_in_ref[...]
    copies = []

    def send(source, target):
        copies.append(pltpu.make_async_copy(source, target, sem.at[len(copies)]))
        copies[-1].start()

    if last:
        fast_row = pl.multiple_of(block * (1 - c), block)
        own_half = pl.ds(pl.multiple_of(half * c, half), half)
        own_edge = pl.ds(pl.multiple_of((rows - half) * (1 - c), half), half)
        send(own_ref, out_ref.at[:, :, :, pl.ds(fast_row, block)])
        for n, ref in enumerate(before):
            send(ref, out_ref.at[:, :, pl.ds(n * group, group), pl.ds(slow_row, block)])
        send(own_sum_ref.at[0], img_ref.at[0, pl.ds(half, block)])
        send(own_sum_ref.at[1, own_half], img_ref.at[0, own_edge])
        send(own_sum_ref.at[2], img_ref.at[1, pl.ds(fast_row, block)])

    def chain(g):
        f = offset + g
        cosine, sine = [inside * t for t in turn_tables(turn_ref, f, masks_halo)]
        get = lambda i, p: slow_ref[(i * 2 + p) * group + g]
        fields = raw_fields(get, cosine, sine)
        yield
        fields = yield from inline(lhs_ref[f], fields, lambda: level_masks(levt_ref[0], levels), block)
        outer = split_fields(fields)
        yield
        fields = yield from crossline(lhs_ref[f], *ordered(c == 0, saved(edge_ref, f), outer), masks_edge, block)
        sum_ref[0] += image_of(fields)
        cosine, sine = [keep * t for t in turn_tables(turn_ref, f, masks_edge)]
        fields = [rotate(field, cosine, sine) for field in fields]
        yield
        if last and g == group - 1:
            own_row = pl.multiple_of(half * (1 - c), half)
            edge_row = pl.multiple_of((rows - half) * c, half)
            send(sum_ref.at[0, pl.ds(own_row, half)], img_ref.at[0, pl.ds(edge_row, half)])
        fields = yield from inline(lhs_ref[f], fields, lambda: level_masks(levt_ref[1], levels), block)
        outer = split_fields(fields)
        yield

        def done(i, real, imag):
            put_done(done_ref, g, i, real, imag)
            if last:
                send(done_ref.at[i, :, g], out_ref.at[i, :, f, pl.ds(slow_row, block)])

        last_pair = ordered(c == 0, saved(mid_ref, f), outer)
        fields = yield from crossline(lhs_ref[f], *last_pair, masks_near, block, done)
        sum_ref[1] += image_of(fields)

    interleave([chain(g) for g in range(group)], SKEW)
    if last:
        send(sum_ref.at[1], img_ref.at[1, pl.ds(slow_row, block)])
    for copy in copies:
        copy.wait()


VMEM = pl.BlockSpec(memory_space=pltpu.VMEM)
SMEM = pl.BlockSpec(memory_space=pltpu.SMEM)
ANY = pl.BlockSpec(memory_space=pl.ANY)
LIMIT = 48 * 1024 * 1024
SKEW = 3
SKEW1 = 2
LAG = 1
GROUPS = 2


def on_device(waves, levels, coeffs, angles, order):
    freqs = order.shape[0]
    rows, width = levels.shape
    level_count, taps = coeffs.shape[2:]
    block = taps - 1
    count = lax.axis_size("strip")
    index = lax.axis_index("strip")
    c = index % 2
    groups = GROUPS if freqs % GROUPS == 0 else 1
    group = freqs // groups

    def side(cells, start, low=0, high=freqs):
        cells = lax.dynamic_slice_in_dim(cells, start, block, axis=3)
        return cells[:, :, low:high].reshape(-1, block, width)

    shots = lax.axis_size("shot")
    across, within = [], []
    for shot in range(shots):
        for i in range(count):
            j = i + 1 if i % 2 else i - 1
            other = shot if 0 <= j < count else min(shot ^ 1, shots - 1)
            across.append((shot * count + i, other * count + (j if 0 <= j < count else i)))
            within.append((shot * count + i, shot * count + (i ^ 1)))
    axes = ("shot", "strip")

    slow_row, fast_row = c * (rows - block), (1 - c) * (rows - block)
    slow = [lax.ppermute(side(waves, slow_row, 0, group), axes, across)]
    near = side(waves, fast_row)
    fast = lax.ppermute(near, axes, within)
    cells, marks, _ = lax.optimization_barrier((waves, levels, near))
    fast_levels = lax.ppermute(lax.dynamic_slice_in_dim(marks, fast_row, block, axis=0), axes, within)
    slow_levels = lax.ppermute(lax.dynamic_slice_in_dim(marks, slow_row, block, axis=0), axes, across)
    for g in range(1, groups):
        slow.append(lax.ppermute(side(cells, slow_row, g * group, (g + 1) * group), axes, across))

    meta = jnp.concatenate([jnp.cos(angles).ravel(), jnp.sin(angles).ravel(), order.astype(F32)])
    lhs_shape = (freqs, 2 * level_count * block, 2 * LANES)
    state = (freqs, 2, 2, 2, block, width)
    dots = 16 * freqs * 2 * lhs_shape[1] * 12 * block * width
    own_done, own_sum, edge, middle, lhs, tiles = pl.pallas_call(
        first_kernel,
        out_shape=[
            jax.ShapeDtypeStruct((2, 2, freqs, block, width), F32),
            jax.ShapeDtypeStruct((3, block, width), F32),
            jax.ShapeDtypeStruct(state, BF16),
            jax.ShapeDtypeStruct(state, BF16),
            jax.ShapeDtypeStruct(lhs_shape, BF16),
            jax.ShapeDtypeStruct((freqs, 2, level_count, 8, LANES), F32),
        ],
        in_specs=[SMEM, VMEM, VMEM, VMEM, VMEM, VMEM],
        out_specs=[VMEM] * 6,
        scratch_shapes=[
            pltpu.VMEM(coeffs.shape[:2] + (8, LANES), F32),
            pltpu.VMEM((2 * block, width), F32),
            pltpu.VMEM((5, LANES, LANES), F32),
        ],
        compiler_params=pltpu.CompilerParams(vmem_limit_bytes=LIMIT),
        cost_estimate=pl.CostEstimate(flops=2 * dots, bytes_accessed=8 << 20, transcendentals=0),
        name="own_rows",
    )(meta, coeffs, waves, levels, fast, fast_levels)
    total, parts = [], []
    for g in range(groups):
        last = g == groups - 1
        args = [slow[g], slow_levels, levels, lhs, tiles, edge, middle, *total]
        shapes = [(2, block, width), (2, 2, group, block, width)]
        scratch = [pltpu.VMEM((2 * block, width), F32), pltpu.VMEM((2, LANES, LANES), F32)]
        outs = shapes
        if last:
            args += [own_done, own_sum, *parts]
            outs = [waves.shape, (STEPS, rows, width)]
            scratch = [pltpu.VMEM(shape, F32) for shape in shapes] + scratch
            scratch.append(pltpu.SemaphoreType.DMA((groups + 2 * group + 5,)))
        result = pl.pallas_call(
            functools.partial(second_kernel, g * group, g == 0, last),
            out_shape=[jax.ShapeDtypeStruct(shape, F32) for shape in outs],
            in_specs=[VMEM] * len(args),
            out_specs=[ANY if last else VMEM] * len(outs),
            scratch_shapes=scratch,
            compiler_params=pltpu.CompilerParams(vmem_limit_bytes=LIMIT),
            cost_estimate=pl.CostEstimate(flops=dots // groups, bytes_accessed=4 << 20, transcendentals=0),
            name=f"edge_rows_{g}",
        )(*args)
        total = result[:1]
        parts.append(result[1])
    return tuple(result)


def solution(mesh):
    in_specs = (P(None, None, "shot", "strip", None), P("strip", None), P(), P(), P("shot"))
    out_specs = (P(None, None, "shot", "strip", None), P("shot", "strip", None))
    return jax.shard_map(
        on_device, mesh=mesh, in_specs=in_specs, out_specs=out_specs, check_vma=False
    )
```

```python
import functools

import jax
import jax.numpy as jnp
from jax import lax
from jax.experimental import pallas as pl
from jax.experimental.pallas import tpu as pltpu
from jax.sharding import PartitionSpec as P

STEPS = 2
LANES = 128
F32 = jnp.float32
BF16 = jnp.bfloat16


def pick(values, masks):
    out = values[0]
    for value, mask in zip(values[1:], masks):
        out = jnp.where(mask, value, out)
    return out


def level_masks(level, count):
    return [level == float(l) for l in range(1, count)]


def split(cells):
    high = cells.astype(BF16)
    return high, (cells - high.astype(F32)).astype(BF16)


def build_filters(coef_ref, row_of, pad_ref, lhs_ref, wanted, block):
    levels, taps = coef_ref.shape[2:]
    pad_ref[...] = jnp.zeros_like(pad_ref)
    pad_ref[:, :, :levels, :taps] = coef_ref[...]
    wide = 2 * block
    for n, f in enumerate(wanted):
        row = row_of(f)
        real, imag = pad_ref[0, row], pad_ref[1, row]
        tables = (real - pltpu.roll(imag, wide, 1), imag + pltpu.roll(real, wide, 1))
        tables = [table + pltpu.roll(table, 2 * wide, 1) for table in tables]
        for level in range(levels):
            for part in range(2):
                line = jnp.broadcast_to(tables[part][level : level + 1], (block, LANES))
                high, low = split(pltpu.roll(line, 0, 1, stride=1, stride_axis=0))
                at = (level * 2 + part) * block
                lhs_ref[n, at : at + block, :LANES] = high
                lhs_ref[n, at : at + block, LANES:] = low


def band_product(lhs, reals, imags):
    rhs = jnp.concatenate([reals[0], imags[0], reals[1], imags[1], reals[0], imags[0]], axis=0)
    return jnp.dot(lhs[:, : rhs.shape[0]], rhs, preferred_element_type=F32)


def band_pick(found, masks, block):
    count = found.shape[0] // (2 * block)
    return [
        pick([found[(l * 2 + part) * block : (l * 2 + part + 1) * block] for l in range(count)], masks)
        for part in range(2)
    ]


def turn_tables(turn_ref, f, masks):
    height, width = masks[0].shape
    tables = []
    for part in range(2):
        values = []
        for l in range(len(masks) + 1):
            tile = turn_ref[f, part, l]
            tile = jnp.concatenate([tile] * (height // tile.shape[0]), axis=0)
            values.append(jnp.concatenate([tile] * (width // LANES), axis=1))
        tables.append(pick(values, masks))
    return tables


def rotate(cells, cosine, sine):
    real, imag = cells
    return real * cosine - imag * sine, real * sine + imag * cosine


def to_columns(fields, block):
    chunks = fields[0].shape[1] // LANES
    return jnp.concatenate(
        [field[:, c * LANES : (c + 1) * LANES] for c in range(chunks) for field in fields], axis=0
    ).T


def inline(lhs, fields, masks_t, block):
    half = block // 2
    count = len(fields)
    chunks = fields[0][0].shape[1] // LANES
    step = count * block
    lane = lax.broadcasted_iota(jnp.int32, (half, LANES), 1)
    columns = []
    for part in range(2):
        columns.append(to_columns([field[part] for field in fields], block))
        yield
    parts = []
    for cols in columns:
        before = jnp.where(lane < step, 0.0, pltpu.roll(cols[LANES - half :], step, 1))
        after = jnp.where(lane >= LANES - step, 0.0, pltpu.roll(cols[:half], LANES - step, 1))
        parts.append(split(jnp.concatenate([before, cols, after], axis=0)))
        yield
    mid = LANES // 2
    halves = [[[], []], [[], []]]
    masks_t = masks_t()
    found = []
    spots = list(range(0, mid, block))

    def finish(at):
        masks = [jnp.concatenate([m[at : at + block], m[mid + at : mid + at + block]], axis=1) for m in masks_t]
        got = band_pick(found.pop(0), masks, block)
        for part in range(2):
            halves[part][0].append(got[part][:, :LANES])
            halves[part][1].append(got[part][:, LANES:])

    for n, at in enumerate(spots):
        windows = [
            [
                jnp.concatenate([x[at : at + 2 * block], x[mid + at : mid + at + 2 * block]], axis=1)
                for x in parts[part]
            ]
            for part in range(2)
        ]
        found.append(band_product(lhs, windows[0], windows[1]))
        yield
        if n >= LAG:
            finish(spots[n - LAG])
    for at in spots[len(spots) - LAG :]:
        finish(at)
    yield
    back = []
    for part in range(2):
        back.append(jnp.concatenate(halves[part][0] + halves[part][1], axis=0).T)
        yield
    return [
        [
            jnp.concatenate(
                [back[part][(c * count + i) * block : (c * count + i + 1) * block] for c in range(chunks)], axis=1
            )
            for part in range(2)
        ]
        for i in range(count)
    ]


def split_fields(fields):
    return [list(zip(*[split(cells) for cells in field])) for field in fields]


def saved(ref, f):
    return [[[ref[f, i, kind, part] for part in range(2)] for kind in range(2)] for i in range(2)]


def save(ref, f, blocks):
    for i in range(2):
        for kind in range(2):
            for part in range(2):
                ref[f, i, kind, part] = blocks[i][kind][part]


def ordered(swap, first, second):
    both = [
        [[(jnp.where(swap, y, x), jnp.where(swap, x, y)) for x, y in zip(p, q)] for p, q in zip(a, b)]
        for a, b in zip(first, second)
    ]
    return [[[[pair[n] for pair in kind] for kind in field] for field in both] for n in range(2)]


def crossline(lhs, first, second, masks, block):
    wide = 2 * LANES
    width = first[0][0][0].shape[1]
    pieces = [[[], []], [[], []]]
    spots = [(i, at) for i in range(2) for at in range(0, width, wide)]
    found = []

    def finish(spot):
        i, at = spot
        got = band_pick(found.pop(0), [m[:, at : at + wide] for m in masks], block)
        for part in range(2):
            pieces[i][part].append(got[part])

    for n, (i, at) in enumerate(spots):
        windows = [
            [
                jnp.concatenate([b[i][kind][part][:, at : at + wide] for b in (first, second)], axis=0)
                for kind in range(2)
            ]
            for part in range(2)
        ]
        found.append(band_product(lhs, windows[0], windows[1]))
        yield
        if n >= LAG:
            finish(spots[n - LAG])
    for spot in spots[len(spots) - LAG :]:
        finish(spot)
    yield
    return [[jnp.concatenate(p, axis=1) for p in piece] for piece in pieces]


def interleave(chains, skew):
    live = dict(enumerate(chains))
    tick = 0
    while live:
        for n in list(live):
            if tick >= n * skew and next(live[n], live) is live:
                del live[n]
        tick += 1


def image_of(fields):
    (sr, si), (qr, qi) = fields
    return sr * qr - si * qi


def raw_fields(get, cosine, sine):
    fields = [[get(i, p) for p in range(2)] for i in range(2)]
    fields[1][1] = -fields[1][1]
    return [rotate(field, cosine, sine) for field in fields]


def put_done(done_ref, f, fields):
    (sr, si), (qr, qi) = fields
    done_ref[0, 0, f], done_ref[0, 1, f], done_ref[1, 0, f], done_ref[1, 1, f] = sr, si, qr, -qi


def window_levels(ref, inner, outer, inner_at, block):
    ref[pl.ds(pl.multiple_of(inner_at, block), block)] = inner
    ref[pl.ds(pl.multiple_of(block - inner_at, block), block)] = outer
    return ref[block // 2 : block // 2 + block]


def first_kernel(
    meta_ref, coef_ref, waves_ref, lev_ref, fast_ref, halo_ref,
    done_ref, acc_ref, edge_ref, mid_ref, lhs_ref, turn_ref,
    pad_ref, levw_ref, levt_ref,
):
    freqs = lhs_ref.shape[0]
    levels, taps = coef_ref.shape[2:]
    block = taps - 1
    half = block // 2
    c = lax.axis_index("strip") % 2

    def row_of(f):
        return meta_ref[2 * freqs * levels + f].astype(jnp.int32)

    for f in range(freqs):
        for part in range(2):
            for l in range(levels):
                turn_ref[f, part, l] = jnp.full(turn_ref.shape[3:], meta_ref[(part * freqs + row_of(f)) * levels + l], F32)
    build_filters(coef_ref, row_of, pad_ref, lhs_ref, range(freqs), block)
    slow_row = pl.multiple_of(block * c, block)
    fast_row = pl.multiple_of(block * (1 - c), block)
    lev_slow = lev_ref[pl.ds(slow_row, block)].astype(F32)
    lev_fast = lev_ref[pl.ds(fast_row, block)].astype(F32)
    lev_halo = halo_ref[...].astype(F32)
    lev_mid = lev_ref[half : half + block].astype(F32)
    lev_edge = window_levels(levw_ref, lev_fast, lev_halo, block * c, block)
    blocks = (lev_slow, lev_fast, lev_halo, lev_mid, lev_edge)
    for slot, lev in enumerate(blocks):
        levt_ref[slot] = to_columns([lev, lev], block)
    masks = [level_masks(lev, levels) for lev in blocks]
    acc_ref[...] = jnp.zeros_like(acc_ref)
    ready = {}

    def start_chain(f, slot):
        cosine, sine = turn_tables(turn_ref, f, masks[slot])
        if slot < 2:
            at = (slow_row, fast_row)[slot]
            get = lambda i, p: waves_ref[i, p, f, pl.ds(at, block)]
        else:
            get = lambda i, p: fast_ref[(i * 2 + p) * freqs + f]
        fields = raw_fields(get, cosine, sine)
        yield
        fields = yield from inline(lhs_ref[f], fields, lambda: level_masks(levt_ref[slot], levels), block)
        ready[f, slot] = split_fields(fields)
        if slot == 0:
            save(edge_ref, f, ready[f, slot])

    def next_chain(f, slot):
        first, second = ((0, 1), (1, 2))[slot]
        fields = yield from crossline(lhs_ref[f], *ordered(c == 1, ready[f, first], ready[f, second]), masks[3 + slot], block)
        acc_ref[slot] += image_of(fields)
        cosine, sine = turn_tables(turn_ref, f, masks[3 + slot])
        fields = [rotate(field, cosine, sine) for field in fields]
        yield
        fields = yield from inline(lhs_ref[f], fields, lambda: level_masks(levt_ref[3 + slot], levels), block)
        ready[f, 3 + slot] = split_fields(fields)
        if slot == 0:
            save(mid_ref, f, ready[f, 3])

    def last_chain(f):
        fields = yield from crossline(lhs_ref[f], *ordered(c == 1, ready[f, 3], ready[f, 4]), masks[1], block)
        acc_ref[2] += image_of(fields)
        put_done(done_ref, f, fields)

    interleave([start_chain(f, slot) for f in range(freqs) for slot in range(3)], SKEW1)
    interleave([next_chain(f, slot) for f in range(freqs) for slot in range(2)], SKEW1)
    interleave([last_chain(f) for f in range(freqs)], SKEW1)


def second_kernel(
    offset, first, last,
    slow_ref, halo_ref, lev_ref, lhs_ref, turn_ref, edge_ref, mid_ref, *refs,
):
    refs = list(refs)
    sum_in_ref = None if first else refs.pop(0)
    if last:
        out_ref, img_ref, sum_ref, done_ref, levw_ref, levt_ref, sem = refs[-7:]
        own_ref, own_sum_ref, *before = refs[:-7]
    else:
        sum_ref, done_ref, levw_ref, levt_ref = refs
    levels = turn_ref.shape[2]
    block = lhs_ref.shape[1] // (2 * levels)
    group = done_ref.shape[2]
    half = block // 2
    rows = lev_ref.shape[0]
    index = lax.axis_index("strip")
    c = index % 2
    outside = jnp.where(c == 0, index == 0, index == lax.axis_size("strip") - 1)
    inside = jnp.where(outside, 0.0, 1.0).astype(F32)
    slow_row = pl.multiple_of(block * c, block)
    lev_near = lev_ref[pl.ds(slow_row, block)].astype(F32)
    lev_halo = halo_ref[...].astype(F32)
    lev_edge = window_levels(levw_ref, lev_near, lev_halo, block * (1 - c), block)
    for slot, lev in enumerate((lev_halo, lev_edge)):
        levt_ref[slot] = to_columns([lev, lev], block)
    masks_near, masks_halo, masks_edge = [level_masks(lev, levels) for lev in (lev_near, lev_halo, lev_edge)]
    line = lax.broadcasted_iota(jnp.int32, lev_edge.shape, 0)
    keep = jnp.where((line >= half) == (c == 0), 1.0, inside)
    sum_ref[...] = jnp.zeros_like(sum_ref) if first else sum_in_ref[...]
    copies = []

    def send(source, target):
        copies.append(pltpu.make_async_copy(source, target, sem.at[len(copies)]))
        copies[-1].start()

    if last:
        fast_row = pl.multiple_of(block * (1 - c), block)
        own_half = pl.ds(pl.multiple_of(half * c, half), half)
        own_edge = pl.ds(pl.multiple_of((rows - half) * (1 - c), half), half)
        send(own_ref, out_ref.at[:, :, :, pl.ds(fast_row, block)])
        for n, ref in enumerate(before):
            send(ref, out_ref.at[:, :, pl.ds(n * group, group), pl.ds(slow_row, block)])
        send(own_sum_ref.at[0], img_ref.at[0, pl.ds(half, block)])
        send(own_sum_ref.at[1, own_half], img_ref.at[0, own_edge])
        send(own_sum_ref.at[2], img_ref.at[1, pl.ds(fast_row, block)])

    def chain(g):
        f = offset + g
        cosine, sine = [inside * t for t in turn_tables(turn_ref, f, masks_halo)]
        get = lambda i, p: slow_ref[(i * 2 + p) * group + g]
        fields = raw_fields(get, cosine, sine)
        yield
        fields = yield from inline(lhs_ref[f], fields, lambda: level_masks(levt_ref[0], levels), block)
        outer = split_fields(fields)
        yield
        fields = yield from crossline(lhs_ref[f], *ordered(c == 0, saved(edge_ref, f), outer), masks_edge, block)
        sum_ref[0] += image_of(fields)
        cosine, sine = [keep * t for t in turn_tables(turn_ref, f, masks_edge)]
        fields = [rotate(field, cosine, sine) for field in fields]
        yield
        if last and g == group - 1:
            own_row = pl.multiple_of(half * (1 - c), half)
            edge_row = pl.multiple_of((rows - half) * c, half)
            send(sum_ref.at[0, pl.ds(own_row, half)], img_ref.at[0, pl.ds(edge_row, half)])
        fields = yield from inline(lhs_ref[f], fields, lambda: level_masks(levt_ref[1], levels), block)
        outer = split_fields(fields)
        yield
        fields = yield from crossline(lhs_ref[f], *ordered(c == 0, saved(mid_ref, f), outer), masks_near, block)
        sum_ref[1] += image_of(fields)
        put_done(done_ref, g, fields)
        if last:
            send(done_ref.at[:, :, g], out_ref.at[:, :, f, pl.ds(slow_row, block)])

    interleave([chain(g) for g in range(group)], SKEW)
    if last:
        send(sum_ref.at[1], img_ref.at[1, pl.ds(slow_row, block)])
    for copy in copies:
        copy.wait()


VMEM = pl.BlockSpec(memory_space=pltpu.VMEM)
SMEM = pl.BlockSpec(memory_space=pltpu.SMEM)
ANY = pl.BlockSpec(memory_space=pl.ANY)
LIMIT = 48 * 1024 * 1024
SKEW = 4
SKEW1 = 2
LAG = 1
GROUPS = 2


def on_device(waves, levels, coeffs, angles, order):
    freqs = order.shape[0]
    rows, width = levels.shape
    level_count, taps = coeffs.shape[2:]
    block = taps - 1
    count = lax.axis_size("strip")
    index = lax.axis_index("strip")
    c = index % 2
    groups = GROUPS if freqs % GROUPS == 0 else 1
    group = freqs // groups

    def side(cells, start, low=0, high=freqs):
        cells = lax.dynamic_slice_in_dim(cells, start, block, axis=3)
        return cells[:, :, low:high].reshape(-1, block, width)

    shots = lax.axis_size("shot")
    across, within = [], []
    for shot in range(shots):
        for i in range(count):
            j = i + 1 if i % 2 else i - 1
            other = shot if 0 <= j < count else min(shot ^ 1, shots - 1)
            across.append((shot * count + i, other * count + (j if 0 <= j < count else i)))
            within.append((shot * count + i, shot * count + (i ^ 1)))
    axes = ("shot", "strip")

    slow_row, fast_row = c * (rows - block), (1 - c) * (rows - block)
    slow = [lax.ppermute(side(waves, slow_row, 0, group), axes, across)]
    near = side(waves, fast_row)
    fast = lax.ppermute(near, axes, within)
    cells, marks, _ = lax.optimization_barrier((waves, levels, near))
    fast_levels = lax.ppermute(lax.dynamic_slice_in_dim(marks, fast_row, block, axis=0), axes, within)
    slow_levels = lax.ppermute(lax.dynamic_slice_in_dim(marks, slow_row, block, axis=0), axes, across)
    for g in range(1, groups):
        slow.append(lax.ppermute(side(cells, slow_row, g * group, (g + 1) * group), axes, across))

    meta = jnp.concatenate([jnp.cos(angles).ravel(), jnp.sin(angles).ravel(), order.astype(F32)])
    lhs_shape = (freqs, 2 * level_count * block, 2 * LANES)
    state = (freqs, 2, 2, 2, block, width)
    dots = 16 * freqs * 2 * lhs_shape[1] * 12 * block * width
    own_done, own_sum, edge, middle, lhs, tiles = pl.pallas_call(
        first_kernel,
        out_shape=[
            jax.ShapeDtypeStruct((2, 2, freqs, block, width), F32),
            jax.ShapeDtypeStruct((3, block, width), F32),
            jax.ShapeDtypeStruct(state, BF16),
            jax.ShapeDtypeStruct(state, BF16),
            jax.ShapeDtypeStruct(lhs_shape, BF16),
            jax.ShapeDtypeStruct((freqs, 2, level_count, 8, LANES), F32),
        ],
        in_specs=[SMEM, VMEM, VMEM, VMEM, VMEM, VMEM],
        out_specs=[VMEM] * 6,
        scratch_shapes=[
            pltpu.VMEM(coeffs.shape[:2] + (8, LANES), F32),
            pltpu.VMEM((2 * block, width), F32),
            pltpu.VMEM((5, LANES, LANES), F32),
        ],
        compiler_params=pltpu.CompilerParams(vmem_limit_bytes=LIMIT),
        cost_estimate=pl.CostEstimate(flops=2 * dots, bytes_accessed=8 << 20, transcendentals=0),
        name="own_rows",
    )(meta, coeffs, waves, levels, fast, fast_levels)
    total, parts = [], []
    for g in range(groups):
        last = g == groups - 1
        args = [slow[g], slow_levels, levels, lhs, tiles, edge, middle, *total]
        shapes = [(2, block, width), (2, 2, group, block, width)]
        scratch = [pltpu.VMEM((2 * block, width), F32), pltpu.VMEM((2, LANES, LANES), F32)]
        outs = shapes
        if last:
            args += [own_done, own_sum, *parts]
            outs = [waves.shape, (STEPS, rows, width)]
            scratch = [pltpu.VMEM(shape, F32) for shape in shapes] + scratch
            scratch.append(pltpu.SemaphoreType.DMA((groups + group + 5,)))
        result = pl.pallas_call(
            functools.partial(second_kernel, g * group, g == 0, last),
            out_shape=[jax.ShapeDtypeStruct(shape, F32) for shape in outs],
            in_specs=[VMEM] * len(args),
            out_specs=[ANY if last else VMEM] * len(outs),
            scratch_shapes=scratch,
            compiler_params=pltpu.CompilerParams(vmem_limit_bytes=LIMIT),
            cost_estimate=pl.CostEstimate(flops=dots // groups, bytes_accessed=4 << 20, transcendentals=0),
            name=f"edge_rows_{g}",
        )(*args)
        total = result[:1]
        parts.append(result[1])
    return tuple(result)


def solution(mesh):
    in_specs = (P(None, None, "shot", "strip", None), P("strip", None), P(), P(), P("shot"))
    out_specs = (P(None, None, "shot", "strip", None), P("shot", "strip", None))
    return jax.shard_map(
        on_device, mesh=mesh, in_specs=in_specs, out_specs=out_specs, check_vma=False
    )
```
